32 devices in a mesh: groups: 2 (over x), dp: 8 (over z, y), adapter: 2 (over core).
Axes of the slice: x: 2, y: 2, z: 4, core: 2. Of those that a mesh axis runs over, the one named last changes fastest.
Arguments:
- layer_input_rows: bfloat16 [4096, 7168], P(('groups', 'dp', 'adapter')), parts along dimension 0, may hold values from -6 to 6
- output_gradient: bfloat16 [4096, 7168], P(('groups', 'dp', 'adapter')), parts along dimension 0, may hold values from -6 to 6
- routed_adapter_index: int32 [4096, 2], P(('groups', 'dp', 'adapter')), parts along dimension 0, may hold values from 0 to 7, all different within a row; in each aligned block of 128 rows (0 to 127, 128 to 255, ...) at most 64 rows name the same one
- router_gate_weight: float32 [4096, 2], P(('groups', 'dp', 'adapter')), parts along dimension 0, may hold values from 0.1 to 1
- down_factor_weight: bfloat16 [8, 16, 7168], P('adapter'), may hold values from -0.0625 to 0.0625
- up_factor_weight: bfloat16 [8, 16, 7168], P('adapter'), may hold values from -1.5 to 1.5
Outputs:
- input_grad: bfloat16 [4096, 7168], P(('groups', 'dp', 'adapter')), parts along dimension 0
- down_grad: float32 [16, 16, 7168], P(('groups', 'adapter'), None, 'dp'), parts along dimension 0
- up_grad: float32 [16, 16, 7168], P(('groups', 'adapter'), None, 'dp'), parts along dimension 0
The draws below stay inside these ranges and needn't reach their ends.
There are 2 independent parts, one for each index of `groups`. The reference program is written for one: setup_inputs(seed, part) draws one part's arguments, and reference() takes and returns one part's arrays. A program takes and returns all parts, laid end to end along the dimension named above; an argument that names none is the same for every part. Nothing has to cross between parts.
Inputs may be any that keep to these rules, and one draw needn't show every extreme that they name: `routed_adapter_index`: the 2 adapters of a token differ. In each aligned block of 128 rows (the rows of one device) no adapter is named by more than 64 rows, and some adapter reaches 64.
All inputs are finite; a program needn't handle non-finite values.
Results may differ from the reference program's by a relative error of at most 0.013.
Values may be sent and summed in bfloat16 or wider, within the bound.
No kernel may reach another device: no remote copies, remote signals or barrier semaphores. Data moves between devices by JAX's collectives and lax.ppermute only.
A program may use at most 128 MiB of HBM per device.

```python
import math
import jax
import jax.numpy as jnp
import numpy as np
from jax import lax

MODEL_WIDTH = 7168
ADAPTER_RANK = 16
TOP = 2
TOK_DEV = 128
MOST = 64
ADAPTER_TOTAL = 8
TOKENS = 2048


def with_spikes(values, rng, source, target, blocks, factor):
    owner, partner = [(jnp.arange(values.shape[axis_at]) // (values.shape[axis_at] // blocks)).reshape([-1 if axis == axis_at else 1 for axis in range(values.ndim)]) for axis_at in (source, target)]
    chosen = jax.random.permutation(rng, blocks)[partner]
    strong = (owner == chosen) | (owner == (partner + blocks // 2) % blocks)
    return jnp.where(strong, factor * values, values)


def block_levels(key, extent, cuts, smallest, largest):
    gain, own = 1.0, jax.random.fold_in(key, 6)
    for axis_at, parts in cuts:
        draws = jnp.exp(jax.random.uniform(jax.random.fold_in(own, axis_at), (parts,), jnp.float32, smallest / len(cuts), largest / len(cuts)))
        gain = gain * jnp.repeat(draws, extent[axis_at] // parts).reshape([-1 if axis == axis_at else 1 for axis in range(len(extent))])
    return gain


def routed_block(rng, own, number, rows, amount, top, reach, slope):
    sequence = jax.random.permutation(rng, amount)
    heavy_load, usual = portions_of(amount, rows * top, reach, slope, True), portions_of(amount, rows * top, reach, slope, False)
    places = jnp.arange(amount)

    def named(lengths, rotation):
        used = int((lengths > 0).sum())
        fixed = max(1, used // 4)
        shifted = fixed + (places - fixed + rotation * (used - fixed)) % max(1, amount - fixed)
        return jnp.zeros((amount,), jnp.int32).at[sequence[jnp.where(places < fixed, places, shifted)]].set(jnp.asarray(lengths, jnp.int32))

    lengths = jnp.where(number % 4 == 0, named(heavy_load, number // 4), named(usual, number - number // 4 - 1))
    mixed = jax.random.permutation(jax.random.fold_in(own, 3), amount)
    giver, receiver = mixed[0:amount // 2 * 2:2], mixed[1:amount // 2 * 2:2]
    slack = jnp.minimum(lengths[giver] - 1, reach - lengths[receiver]) // 2
    slack = jnp.where((giver == sequence[0]) | (receiver == sequence[0]) | (lengths[receiver] == 0), 0, jnp.maximum(slack, 0))
    shifted = jax.random.randint(jax.random.fold_in(own, 4), (amount // 2,), 0, 1 << 20) % (slack + 1)
    lengths = lengths.at[giver].add(-shifted).at[receiver].add(shifted)
    members = jnp.searchsorted(jnp.cumsum(lengths), jnp.arange(rows * top), side="right").astype(jnp.int32)
    table = members.reshape(top, rows).T
    table = table[jax.random.permutation(jax.random.fold_in(own, 1), rows)]
    rotation = jax.random.randint(jax.random.fold_in(own, 2), (rows, 1), 0, top)
    return jnp.take_along_axis(table, (jnp.arange(top)[None, :] + rotation) % top, axis=1)


def portions_of(count, total, reach, skew, full):
    loads = [(1 << 20) // math.isqrt(rank ** skew) + 1 for rank in range(1, count + 1)]
    largest = reach if full else min(reach, max(-(-total // count), total * loads[0] // sum(loads)))
    least = 1 if total - largest >= count - 1 else 0
    counts, rest = [largest] + [least] * (count - 1), total - largest - least * (count - 1)
    while rest > 0:
        movable = [i for i in range(1, count) if counts[i] < largest] or [i for i in range(1, count) if counts[i] < reach]
        pool, left = sum([loads[i] for i in movable]), rest
        for i in movable:
            more = min(reach - counts[i], max(1, left * loads[i] // pool), rest)
            counts[i] = counts[i] + more
            rest = rest - more
    return np.array(counts)


def bell_draw(rng, dims, scale, most, split=(), dtype=jnp.bfloat16):
    entries = scale * jax.random.normal(rng, dims, jnp.float32)
    if split:
        entries = entries * block_levels(rng, dims, split, -0.22, 0.18)
    return jnp.clip(entries, -most, most).astype(dtype)


def bell_draw_with(key, dims, width, limit, shards, heavy, dtype=jnp.bfloat16):
    array = width * jax.random.normal(key, dims, jnp.float32)
    if shards:
        array = array * block_levels(key, dims, shards, -0.22, 0.18)
    return jnp.clip(with_spikes(array, jax.random.fold_in(key, 3), *heavy), -limit, limit).astype(dtype)


def setup_inputs(seed: int = 0, part: int = 0) -> dict:
    key_of = jax.random.split(jax.random.key(seed), 7)
    own_keys = jax.random.split(jax.random.fold_in(key_of[6], part), 7)
    layer_input_rows = bell_draw(own_keys[0], (TOKENS, MODEL_WIDTH), 1.0, 6.0, ((0, 16),))
    output_gradient = bell_draw_with(own_keys[1], (TOKENS, MODEL_WIDTH), 1.0, 6.0, ((0, 16),), (0, 1, 16, 2.0))
    routed_adapter_index_keys = jax.random.split(jax.random.fold_in(own_keys[2], 1), TOKENS // TOK_DEV)
    routed_adapter_index_turns = jax.random.permutation(jax.random.fold_in(own_keys[2], 3), TOKENS // TOK_DEV)
    routed_adapter_index = jax.vmap(lambda own, number: routed_block(jax.random.fold_in(own_keys[2], 2), own, number, TOK_DEV, ADAPTER_TOTAL, TOP, MOST, 2))(routed_adapter_index_keys, routed_adapter_index_turns).reshape((TOKENS, TOP))
    router_gate_weight = jnp.clip(0.1 + 0.9 * jax.random.uniform(own_keys[3], (TOKENS, TOP), jnp.float32) ** block_levels(own_keys[3], (TOKENS, TOP), ((0, 16),), -0.2, 0.2), 0.1, 1.0)
    down_factor_weight = bell_draw(key_of[4], (ADAPTER_TOTAL, ADAPTER_RANK, MODEL_WIDTH), MODEL_WIDTH ** -0.5, 0.0625, ((0, 2),))
    up_factor_weight = bell_draw(key_of[5], (ADAPTER_TOTAL, ADAPTER_RANK, MODEL_WIDTH), ADAPTER_RANK ** -0.5, 1.5, ((0, 2),))
    return dict(layer_input_rows=layer_input_rows, output_gradient=output_gradient, routed_adapter_index=routed_adapter_index, router_gate_weight=router_gate_weight, down_factor_weight=down_factor_weight, up_factor_weight=up_factor_weight)


def reference(layer_input_rows, output_gradient, routed_adapter_index, router_gate_weight, down_factor_weight, up_factor_weight):
    adapter_span = jnp.arange(ADAPTER_TOTAL).astype(jnp.int32)

    def each_adapter_rows(running, inputs):
        down_w, up_w, which = inputs
        weight = jnp.sum(jnp.where(routed_adapter_index == which, router_gate_weight, 0.0), axis=1)
        scaled = (weight[:, None] * output_gradient.astype(jnp.float32)).astype(jnp.bfloat16)
        low_grad = jnp.dot(scaled, up_w.T, preferred_element_type=jnp.float32).astype(jnp.bfloat16)
        row_grad = jnp.dot(low_grad, down_w, preferred_element_type=jnp.float32).astype(jnp.bfloat16)
        running = running + row_grad.astype(jnp.float32)
        down_piece = jnp.dot(low_grad.T, layer_input_rows, preferred_element_type=jnp.float32)
        low_act = jnp.dot(layer_input_rows, down_w.T, preferred_element_type=jnp.float32).astype(jnp.bfloat16)
        up_piece = jnp.dot(low_act.T, scaled, preferred_element_type=jnp.float32)
        return running, (down_piece, up_piece)

    begin_offset = jnp.zeros(output_gradient.shape, jnp.float32)
    total_sum, pieces = lax.scan(each_adapter_rows, begin_offset, (down_factor_weight, up_factor_weight, adapter_span))
    return total_sum.astype(jnp.bfloat16), pieces[0], pieces[1]
```

```python
import jax
import jax.numpy as jnp
from jax import lax
from jax.sharding import PartitionSpec as P

BF16 = jnp.bfloat16
F32 = jnp.float32
SWAP = [(0, 1), (1, 0)]


def routed_weights(ids, gates, first, count, rank):
    column = first + lax.broadcasted_iota(jnp.int32, (1, 1, count), 2)
    weights = jnp.sum(jnp.where(ids[:, :, None] == column, gates[:, :, None], 0.0), axis=1)
    return jnp.repeat(weights, rank, axis=1)


def reduce_over_dp(down, up):
    replicas = lax.axis_size("dp")
    both = jnp.concatenate([down, up], axis=0)
    rows, width = both.shape
    block = width // replicas
    if replicas & (replicas - 1) or replicas < 2:
        return lax.psum_scatter(both.astype(F32), "dp", scatter_dimension=1, tiled=True)
    me = lax.axis_index("dp")
    far, near = me // 2, me % 2
    total = None
    for step in reversed(range(replicas // 2)):
        base = (far ^ step) * 2
        send = lax.dynamic_slice(both, (0, (base + 1 - near) * block), (rows, block))
        keep = lax.dynamic_slice(both, (0, (base + near) * block), (rows, block))
        came = lax.ppermute(send, "dp", [(i, i ^ 1) for i in range(replicas)])
        term = keep.astype(F32) + came.astype(F32)
        if step:
            term = lax.ppermute(
                term.astype(BF16), "dp", [(i, i ^ (2 * step)) for i in range(replicas)]
            ).astype(F32)
        total = term if total is None else total + term
    return total


def shards(x, g, ids, gates, down_w, up_w):
    tokens, width = x.shape
    count, rank, _ = down_w.shape
    core = lax.axis_index("adapter")
    a = down_w.reshape(count * rank, width)
    b = up_w.reshape(count * rank, width)
    own_weight = routed_weights(ids, gates, core * count, count, rank)
    other_weight = routed_weights(ids, gates, (1 - core) * count, count, rank)
    weight_in = lax.ppermute(other_weight, "adapter", SWAP)
    g_in = lax.ppermute(g, "adapter", SWAP)
    x_in = lax.ppermute(x, "adapter", SWAP)
    a_in = lax.ppermute(a, "adapter", SWAP)

    def low(rows, factor, weight):
        z = lax.dot_general(rows, factor, (((1,), (1,)), ((), ())), preferred_element_type=F32)
        return (z * weight).astype(BF16)

    def outer(left, right):
        return lax.dot_general(left, right, (((0,), (0,)), ((), ())), preferred_element_type=F32)

    low_grad = low(g, b, own_weight)
    low_grad_in = low(g_in, b, weight_in)
    low_act = low(x, a, own_weight)
    low_act_in = low(x_in, a, weight_in)
    down = (outer(low_grad, x) + outer(low_grad_in, x_in)).astype(BF16)
    up = (outer(low_act, g) + outer(low_act_in, g_in)).astype(BF16)
    low_grad_back = lax.ppermute(low_grad_in, "adapter", SWAP)
    input_grad = (
        jnp.dot(low_grad, a, preferred_element_type=F32)
        + jnp.dot(low_grad_back, a_in, preferred_element_type=F32)
    ).astype(BF16)
    both = reduce_over_dp(down, up).reshape(2, count, rank, -1)
    return input_grad, both[0], both[1]


def solution(mesh):
    tok = P(("groups", "dp", "adapter"), None)
    return jax.shard_map(
        shards,
        mesh=mesh,
        in_specs=(tok, tok, tok, tok, P("adapter", None, None), P("adapter", None, None)),
        out_specs=(
            tok,
            P(("groups", "adapter"), None, "dp"),
            P(("groups", "adapter"), None, "dp"),
        ),
        check_vma=False,
    )
```

```python
import functools

import jax
import jax.numpy as jnp
from jax import lax
from jax.experimental import pallas as pl
from jax.experimental.pallas import tpu as pltpu
from jax.sharding import PartitionSpec as P

BF16 = jnp.bfloat16
F32 = jnp.float32
SWAP = [(0, 1), (1, 0)]
VMEM_LIMIT = 40 * 1024 * 1024
NT = (((1,), (1,)), ((), ()))
TN = (((0,), (0,)), ((), ()))


def params():
    return pltpu.CompilerParams(vmem_limit_bytes=VMEM_LIMIT)


def cost(flops, moved):
    return pl.CostEstimate(flops=int(flops), bytes_accessed=int(moved), transcendentals=0)


def whole(shape):
    return pl.BlockSpec(shape, lambda *_: (0,) * len(shape))


def steps_of(width):
    for steps in (4, 7, 2):
        if width % (steps * 128) == 0:
            return steps
    return 1


def gate_columns(core_ref, ids, gates, rows, rank):
    adapter = lax.broadcasted_iota(jnp.int32, (rows, ids.shape[1]), 0) // rank
    adapter = adapter + core_ref[0] * (rows // rank)
    total = jnp.zeros((rows, ids.shape[1]), F32)
    for k in range(ids.shape[0]):
        total = total + jnp.where(ids[k : k + 1, :] == adapter, gates[k : k + 1, :], 0.0)
    return total


def low_kernel(rank, count, core_ref, ids_ref, gates_ref, *refs):
    pairs, outs, sums = refs[: 2 * count], refs[2 * count : 3 * count], refs[3 * count :]
    step = pl.program_id(0)
    for j in range(count):
        part = lax.dot_general(
            pairs[2 * j][...], pairs[2 * j + 1][...], NT, preferred_element_type=F32
        )

        @pl.when(step == 0)
        def _():
            sums[j][...] = part

        @pl.when(step > 0)
        def _():
            sums[j][...] += part

    @pl.when(step == pl.num_programs(0) - 1)
    def _():
        weight = gate_columns(core_ref, ids_ref[...], gates_ref[...], sums[0].shape[0], rank)
        for j in range(count):
            outs[j][...] = (sums[j][...] * weight).astype(BF16)


def low_products(core, ids, gates, rank, *pairs):
    count = len(pairs)
    rows, width = pairs[0][0].shape
    tokens = pairs[0][1].shape[0]
    steps = steps_of(width)
    tile = width // steps
    along = lambda extent: pl.BlockSpec((extent, tile), lambda s, *_: (0, s))
    return pl.pallas_call(
        functools.partial(low_kernel, rank, count),
        grid_spec=pltpu.PrefetchScalarGridSpec(
            num_scalar_prefetch=1,
            grid=(steps,),
            in_specs=[whole(ids.shape), whole(gates.shape)] + [along(rows), along(tokens)] * count,
            out_specs=[whole((rows, tokens))] * count,
            scratch_shapes=[pltpu.VMEM((rows, tokens), F32)] * count,
        ),
        out_shape=[jax.ShapeDtypeStruct((rows, tokens), BF16)] * count,
        compiler_params=params(),
        cost_estimate=cost(
            2 * count * rows * tokens * width, count * 2 * (rows + tokens) * width
        ),
    )(core, ids, gates, *(array for pair in pairs for array in pair))


def piece_kernel(block, where_ref, lg_ref, lgi_ref, la_ref, lai_ref, x_ref, xi_ref, g_ref, gi_ref,
                 send_ref, keep_ref):
    near = where_ref[1]
    rows = lg_ref.shape[0]

    def columns(start):
        cols = pl.ds(pl.multiple_of(start, 128), block)
        dot = functools.partial(jnp.dot, preferred_element_type=F32)
        down = dot(lg_ref[...], x_ref[:, cols]) + dot(lgi_ref[...], xi_ref[:, cols])
        up = dot(la_ref[...], g_ref[:, cols]) + dot(lai_ref[...], gi_ref[:, cols])
        return down, up

    down, up = columns((1 - near) * block)
    send_ref[:rows, :] = down.astype(BF16)
    send_ref[rows:, :] = up.astype(BF16)
    down, up = columns(near * block)
    keep_ref[:rows, :] = down
    keep_ref[rows:, :] = up


def piece(where, low, x, x_in, g, g_in, block):
    rows = low[0].shape[0]
    tokens = x.shape[0]
    tall = pl.BlockSpec((tokens, 2 * block), lambda s, where: (0, where[0]))
    return pl.pallas_call(
        functools.partial(piece_kernel, block),
        grid_spec=pltpu.PrefetchScalarGridSpec(
            num_scalar_prefetch=1,
            grid=(1,),
            in_specs=[whole(low[0].shape)] * 4 + [tall] * 4,
            out_specs=[whole((2 * rows, block))] * 2,
        ),
        out_shape=[
            jax.ShapeDtypeStruct((2 * rows, block), BF16),
            jax.ShapeDtypeStruct((2 * rows, block), F32),
        ],
        compiler_params=params(),
        cost_estimate=cost(
            16 * rows * tokens * block, 16 * tokens * block + 12 * rows * block
        ),
    )(where, *low, x, x_in, g, g_in)


def add_kernel(keep_ref, came_ref, out_ref):
    out_ref[...] = (keep_ref[...] + came_ref[...].astype(F32)).astype(out_ref.dtype)


def add(keep, came):
    return pl.pallas_call(
        add_kernel,
        out_shape=jax.ShapeDtypeStruct(keep.shape, BF16),
        compiler_params=params(),
        cost_estimate=cost(keep.size, 8 * keep.size),
    )(keep, came)


def last_kernel(count, keep_ref, *refs):
    came, (down_ref, up_ref) = refs[:count], refs[count:]
    total = keep_ref[...]
    for ref in came:
        total = total + ref[...].astype(F32)
    rows = down_ref.shape[0]
    down_ref[...] = total[:rows]
    up_ref[...] = total[rows:]


def last(keep, came):
    rows, block = keep.shape[0] // 2, keep.shape[1]
    return pl.pallas_call(
        functools.partial(last_kernel, len(came)),
        out_shape=[jax.ShapeDtypeStruct((rows, block), F32)] * 2,
        compiler_params=params(),
        cost_estimate=cost(keep.size * len(came), keep.size * (8 + 2 * len(came))),
    )(keep, *came)


def input_kernel(lg_ref, lgo_ref, a_ref, ao_ref, out_ref):
    dot = functools.partial(lax.dot_general, dimension_numbers=TN, preferred_element_type=F32)
    out_ref[...] = (dot(lg_ref[...], a_ref[...]) + dot(lgo_ref[...], ao_ref[...])).astype(BF16)


def input_gradient(low_own, low_other, a, a_other):
    rows, tokens = low_own.shape
    width = a.shape[1]
    steps = steps_of(width)
    tile = width // steps
    return pl.pallas_call(
        input_kernel,
        grid=(steps,),
        in_specs=[whole((rows, tokens))] * 2 + [pl.BlockSpec((rows, tile), lambda s: (0, s))] * 2,
        out_specs=pl.BlockSpec((tokens, tile), lambda s: (0, s)),
        out_shape=jax.ShapeDtypeStruct((tokens, width), BF16),
        compiler_params=params(),
        cost_estimate=cost(4 * rows * tokens * width, 2 * (2 * rows + tokens) * width),
    )(low_own, low_other, a, a_other)


def shards(x, g, ids, gates, down_w, up_w):
    tokens, width = x.shape
    count, rank, _ = down_w.shape
    rows = count * rank
    replicas = lax.axis_size("dp")
    block = width // replicas
    core = lax.axis_index("adapter").astype(jnp.int32).reshape(1)
    a = down_w.reshape(rows, width)
    b = up_w.reshape(rows, width)
    ids, gates = ids.T, gates.T
    swap = lambda array: lax.ppermute(array, "adapter", SWAP)
    g_in, x_in, ids_in, gates_in, a_in = swap(g), swap(x), swap(ids), swap(gates), swap(a)

    lg, la = low_products(core, ids, gates, rank, (b, g), (a, x))
    (lg_in,) = low_products(core, ids_in, gates_in, rank, (b, g_in))
    (la_in,) = low_products(core, ids_in, gates_in, rank, (a, x_in))

    lg_back = swap(lg_in)
    low = (lg, lg_in, la, la_in)
    if replicas >= 2 and replicas & (replicas - 1) == 0 and block % 128 == 0:
        me = lax.axis_index("dp").astype(jnp.int32)
        far, near = me // 2, me % 2
        came = []
        for step in reversed(range(replicas // 2)):
            where = jnp.stack([far ^ step, near])
            send, keep = piece(where, low, x, x_in, g, g_in, block)
            got = lax.ppermute(send, "dp", [(i, i ^ 1) for i in range(replicas)])
            if step:
                term = add(keep, got)
                perm = [(i, i ^ (2 * step)) for i in range(replicas)]
                came.append(lax.ppermute(term, "dp", perm))
            else:
                came.append(got)
        down, up = last(keep, came)
    else:
        dot = functools.partial(jnp.dot, preferred_element_type=F32)
        both = jnp.concatenate([dot(lg, x) + dot(lg_in, x_in), dot(la, g) + dot(la_in, g_in)], axis=0)
        both = lax.psum_scatter(both, "dp", scatter_dimension=1, tiled=True)
        down, up = both[:rows], both[rows:]
    input_grad = input_gradient(lg, lg_back, a, a_in)
    return input_grad, down.reshape(count, rank, block), up.reshape(count, rank, block)


def solution(mesh):
    tok = P(("groups", "dp", "adapter"), None)
    return jax.shard_map(
        shards,
        mesh=mesh,
        in_specs=(tok, tok, tok, tok, P("adapter", None, None), P("adapter", None, None)),
        out_specs=(
            tok,
            P(("groups", "adapter"), None, "dp"),
            P(("groups", "adapter"), None, "dp"),
        ),
        check_vma=False,
    )
```

```python
import functools

import jax
import jax.numpy as jnp
from jax import lax
from jax.experimental import pallas as pl
from jax.experimental.pallas import tpu as pltpu
from jax.sharding import PartitionSpec as P

BF16 = jnp.bfloat16
F32 = jnp.float32
SWAP = [(0, 1), (1, 0)]
VMEM_LIMIT = 12 * 1024 * 1024
HOLD_LIMIT = 50 * 1024 * 1024
VECTORS = pl.BlockSpec(memory_space=pltpu.VMEM)
ANYWHERE = pl.BlockSpec(memory_space=pl.ANY)
SCALARS = pl.BlockSpec(memory_space=pltpu.SMEM)
NT = (((1,), (1,)), ((), ()))
TN = (((0,), (0,)), ((), ()))


def params(limit=VMEM_LIMIT):
    return pltpu.CompilerParams(vmem_limit_bytes=limit)


def cost(flops, moved):
    return pl.CostEstimate(flops=int(flops), bytes_accessed=int(moved), transcendentals=0)


def steps_of(width):
    for steps in (4, 7, 2):
        if width % (steps * 128) == 0:
            return steps
    return 1


def hold_kernel(*refs):
    count = len(refs) // 2
    sources, targets, sems = refs[:count], refs[count:-1], refs[-1]
    copies = [
        pltpu.make_async_copy(source.at[:, cols], target.at[:, cols], sems.at[i, j])
        for i, (source, target) in enumerate(zip(sources, targets))
        for j, cols in enumerate(tiles(source.shape[1]))
    ]
    for copy in copies:
        copy.start()
    for copy in copies:
        copy.wait()


def hold(*arrays):
    return pl.pallas_call(
        hold_kernel,
        in_specs=[ANYWHERE] * len(arrays),
        out_specs=[VECTORS] * len(arrays),
        out_shape=[jax.ShapeDtypeStruct(array.shape, array.dtype) for array in arrays],
        scratch_shapes=[pltpu.SemaphoreType.DMA((len(arrays), steps_of(arrays[0].shape[1])))],
        compiler_params=params(HOLD_LIMIT),
        cost_estimate=cost(0, sum(4 * array.size for array in arrays)),
        name="hold",
    )(*arrays)


def tiles(width):
    count = steps_of(width)
    return [pl.ds(j * (width // count), width // count) for j in range(count)]


def gate_columns(core, ids, gates, rows, rank):
    total = rows // rank
    row = lax.broadcasted_iota(jnp.int32, (rows, ids.shape[1]), 0)
    adapter = (row // rank + core * (total // 2)) % total
    weight = jnp.zeros((rows, ids.shape[1]), F32)
    for k in range(ids.shape[0]):
        weight = weight + jnp.where(ids[k : k + 1, :] == adapter, gates[k : k + 1, :], 0.0)
    return weight


def store_products(where_ref, at, blocks, lows, outers, send_ref, keep_ref):
    wide = send_ref.shape[1] // blocks
    rows = send_ref.shape[0] // 2
    for j in range(blocks):
        cols = pl.ds(pl.multiple_of(where_ref[at + j] * wide, 128), wide)
        into = pl.ds(j * wide, wide)
        for i, (low, outer) in enumerate(zip(lows, outers)):
            product = jnp.dot(low, outer[:, cols], preferred_element_type=F32).astype(BF16)
            out = pl.ds(i * rows, rows)
            send_ref[out, into] = product[:rows]
            keep_ref[out, into] = product[rows:]


def low_kernel(rank, core_ref, where_ref, ids_ref, gates_ref, b_ref, b_in_ref, a_ref, a_in_ref, g_ref, x_ref,
               lg_ref, la_ref, send_ref, keep_ref):
    rows, width = b_ref.shape
    weight = gate_columns(1 - core_ref[0], ids_ref[...], gates_ref[...], 2 * rows, rank)
    lows = []
    for other, own, tokens, out in ((b_in_ref, b_ref, g_ref, lg_ref), (a_in_ref, a_ref, x_ref, la_ref)):
        sums = [jnp.zeros((rows, tokens.shape[0]), F32)] * 2
        for cols in tiles(width):
            for i, factor in enumerate((other, own)):
                sums[i] = sums[i] + lax.dot_general(
                    factor[:, cols], tokens[:, cols], NT, preferred_element_type=F32
                )
        lows.append((jnp.concatenate(sums, axis=0) * weight).astype(BF16))
        out[...] = lows[-1]
    store_products(where_ref, 0, 1, lows, (x_ref, g_ref), send_ref, keep_ref)


def low_products(core, where, ids, gates, rank, b, b_in, a, a_in, g, x, wide):
    rows, width = b.shape
    tokens = x.shape[0]
    return pl.pallas_call(
        functools.partial(low_kernel, rank),
        in_specs=[SCALARS] * 2 + [VECTORS] * 8,
        out_specs=[VECTORS] * 4,
        out_shape=[jax.ShapeDtypeStruct((2 * rows, tokens), BF16)] * 2
        + [jax.ShapeDtypeStruct((2 * rows, wide), BF16)] * 2,
        compiler_params=params(),
        cost_estimate=cost(8 * rows * tokens * (width + wide), 4 * (2 * rows + tokens) * width),
        name="low",
    )(core, where, ids, gates, b, b_in, a, a_in, g, x)


def rest_kernel(blocks, where_ref, lg_ref, la_ref, x_ref, g_ref, send_ref, keep_ref):
    lows = (lg_ref[...], la_ref[...])
    store_products(where_ref, 1, blocks, lows, (x_ref, g_ref), send_ref, keep_ref)


def rest_products(where, lg, la, x, g, blocks, wide):
    rows = lg.shape[0]
    return pl.pallas_call(
        functools.partial(rest_kernel, blocks),
        in_specs=[SCALARS] + [VECTORS] * 4,
        out_specs=[VECTORS] * 2,
        out_shape=[jax.ShapeDtypeStruct((rows, blocks * wide), BF16)] * 2,
        compiler_params=params(),
        cost_estimate=cost(4 * rows * x.shape[0] * blocks * wide, 8 * rows * blocks * wide),
        name="rest",
    )(where, lg, la, x, g)


def fold_kernel(block, at, where_ref, keep_ref, came_ref, after_ref, send_ref, own_ref):
    near = where_ref[where_ref.shape[0] - 1]
    for place, out in ((1 - near, send_ref), (near, own_ref)):
        cols = pl.ds(pl.multiple_of((2 * at + place) * block, 128), block)
        out[...] = (keep_ref[:, cols].astype(F32) + came_ref[:, cols].astype(F32)).astype(out.dtype)


def fold(where, block, at, keep, came, after):
    rows = keep.shape[0]
    return pl.pallas_call(
        functools.partial(fold_kernel, block, at),
        in_specs=[SCALARS] + [VECTORS] * 2 + [ANYWHERE],
        out_specs=[VECTORS] * 2,
        out_shape=[
            jax.ShapeDtypeStruct((rows, block), BF16),
            jax.ShapeDtypeStruct((rows, block), F32),
        ],
        compiler_params=params(),
        cost_estimate=cost(2 * rows * block, 14 * rows * block),
        name="fold",
    )(where, keep, came, after)


def add_kernel(keep_ref, came_ref, out_ref):
    out_ref[...] = (keep_ref[...] + came_ref[...].astype(F32)).astype(out_ref.dtype)


def add(keep, came):
    return pl.pallas_call(
        add_kernel,
        out_shape=jax.ShapeDtypeStruct(keep.shape, BF16),
        compiler_params=params(),
        cost_estimate=cost(keep.size, 8 * keep.size),
        name="add",
    )(keep, came)


def last_kernel(keep_ref, *refs):
    came, (down_ref, up_ref) = refs[:-2], refs[-2:]
    rows = down_ref.shape[0]
    for half, out in ((0, down_ref), (1, up_ref)):
        own = pl.ds(half * rows, rows)
        total = keep_ref[own, :]
        at = 0
        while at < len(came):
            whole = came[at].shape[0] > rows
            total = total + (came[at][own, :] if whole else came[at + half][...]).astype(F32)
            at += 1 if whole else 2
        out[...] = total


def last(keep, came):
    rows, block = keep.shape[0] // 2, keep.shape[1]
    return pl.pallas_call(
        last_kernel,
        in_specs=[VECTORS] * (1 + len(came)),
        out_specs=[VECTORS] * 2,
        out_shape=[jax.ShapeDtypeStruct((rows, block), F32)] * 2,
        compiler_params=params(),
        cost_estimate=cost(keep.size * len(came), keep.size * (8 + 2 * len(came))),
        name="last",
    )(keep, *came)


def input_kernel(low_ref, own_ref, other_ref, out_ref):
    tile = out_ref.shape[1]
    rows = own_ref.shape[0]
    cols = pl.ds(pl.multiple_of(pl.program_id(0) * tile, 128), tile)
    dot = functools.partial(lax.dot_general, dimension_numbers=TN, preferred_element_type=F32)
    out_ref[...] = (
        dot(low_ref[:rows], other_ref[:, cols]) + dot(low_ref[rows:], own_ref[:, cols])
    ).astype(BF16)


def input_gradient(low, own, other):
    tokens = low.shape[1]
    rows, width = own.shape
    steps = steps_of(width)
    tile = width // steps
    return pl.pallas_call(
        input_kernel,
        grid=(steps,),
        in_specs=[VECTORS] * 3,
        out_specs=pl.BlockSpec((tokens, tile), lambda s: (0, s)),
        out_shape=jax.ShapeDtypeStruct((tokens, width), BF16),
        compiler_params=params(),
        cost_estimate=cost(4 * rows * tokens * width, 2 * (2 * rows + tokens) * width),
        name="input",
    )(low, own, other)


def shards(x, g, ids, gates, down_w, up_w):
    tokens, width = x.shape
    count, rank, _ = down_w.shape
    rows = count * rank
    replicas = lax.axis_size("dp")
    block = width // replicas
    core = lax.axis_index("adapter").astype(jnp.int32).reshape(1)
    a = down_w.reshape(rows, width)
    b = up_w.reshape(rows, width)
    ids, gates = ids.T, gates.T
    swap = lambda array: lax.ppermute(array, "adapter", SWAP)
    b_in = swap(b)
    me = lax.axis_index("dp").astype(jnp.int32)
    far, near = me // 2, me % 2
    flip = lambda array, by: lax.ppermute(array, "dp", [(i, i ^ by) for i in range(replicas)])
    steps = replicas // 2
    if steps < 2 or replicas & (replicas - 1) or block % 128:
        return plain(core, ids, gates, rank, x, g, a, b, swap(a), b_in, swap)

    a_in = swap(a)
    g_held, x_held = hold(g, x)
    order = list(reversed(range(steps)))
    where = jnp.stack([far ^ step for step in order] + [near])
    lg, la, pair, keep = low_products(
        core, where, ids, gates, rank, b, b_in, a, a_in, g_held, x_held, 2 * block
    )
    rest_pair, rest_keep = rest_products(where, lg, la, x_held, g_held, steps - 1, 2 * block)
    terms = (keep, swap(pair)), (rest_keep, swap(rest_pair))
    came = []
    send = la
    for i, step in enumerate(order):
        send, own = fold(where, block, max(i - 1, 0), *terms[min(i, 1)], send)
        got = flip(send, 1)
        came.append(flip(add(own, got), 2 * step) if step else got)
    input_grad = input_gradient(lg, a, a_in)
    input_grad, came[-1] = lax.optimization_barrier((input_grad, came[-1]))
    down, up = last(own, came)
    return input_grad, down.reshape(count, rank, block), up.reshape(count, rank, block)


def plain(core, ids, gates, rank, x, g, a, b, a_in, b_in, swap):
    rows = a.shape[0]
    dot = functools.partial(lax.dot_general, preferred_element_type=F32)
    weight = gate_columns(core[0], ids, gates, 2 * rows, rank)
    both_a, both_b = jnp.concatenate([a, a_in]), jnp.concatenate([b, b_in])
    lg = (dot(both_b, g, NT) * weight).astype(BF16)
    la = (dot(both_a, x, NT) * weight).astype(BF16)
    input_grad = dot(lg, both_a, TN).astype(BF16)
    down = jnp.dot(lg, x, preferred_element_type=F32)
    up = jnp.dot(la, g, preferred_element_type=F32)
    own = jnp.concatenate([down[:rows], up[:rows]])
    other = jnp.concatenate([down[rows:], up[rows:]]).astype(BF16)
    total = lax.psum_scatter(
        own + swap(other).astype(F32), "dp", scatter_dimension=1, tiled=True
    ).reshape(2, rows // rank, rank, -1)
    return input_grad, total[0], total[1]


def solution(mesh):
    tok = P(("groups", "dp", "adapter"), None)
    return jax.shard_map(
        shards,
        mesh=mesh,
        in_specs=(tok, tok, tok, tok, P("adapter", None, None), P("adapter", None, None)),
        out_specs=(
            tok,
            P(("groups", "adapter"), None, "dp"),
            P(("groups", "adapter"), None, "dp"),
        ),
        check_vma=False,
    )
```

```python
import functools

import jax
import jax.numpy as jnp
from jax import lax
from jax.experimental import pallas as pl
from jax.experimental.pallas import tpu as pltpu
from jax.sharding import PartitionSpec as P

BF16 = jnp.bfloat16
F32 = jnp.float32
SWAP = [(0, 1), (1, 0)]
VMEM_LIMIT = 12 * 1024 * 1024
OWN_LIMIT = 48 * 1024 * 1024
VECTORS = pl.BlockSpec(memory_space=pltpu.VMEM)
ANYWHERE = pl.BlockSpec(memory_space=pl.ANY)
SCALARS = pl.BlockSpec(memory_space=pltpu.SMEM)
NT = (((1,), (1,)), ((), ()))
TN = (((0,), (0,)), ((), ()))


def params(limit=VMEM_LIMIT):
    return pltpu.CompilerParams(vmem_limit_bytes=limit)


def cost(flops, moved):
    return pl.CostEstimate(flops=int(flops), bytes_accessed=int(moved), transcendentals=0)


def steps_of(width):
    for steps in (4, 7, 2):
        if width % (steps * 128) == 0:
            return steps
    return 1


def own_kernel(b_hbm, g_hbm, a_hbm, x_hbm, grad_ref, act_ref, g_ref, x_ref, b, a, sems):
    width = g_ref.shape[1]
    halves = ((b_hbm, b, g_hbm, g_ref, grad_ref), (a_hbm, a, x_hbm, x_ref, act_ref))
    copies = [
        [
            pltpu.make_async_copy(source.at[:, cols], target.at[:, cols], sems.at[half, i, j])
            for i, (source, target) in enumerate((refs[:2], refs[2:4]))
        ]
        for half, refs in enumerate(halves)
        for j, cols in enumerate(tiles(width))
    ]
    for pair in copies:
        for copy in pair:
            copy.start()
    for half, (_, factor, _, tokens, out) in enumerate(halves):
        total = jnp.zeros(out.shape, F32)
        for j, cols in enumerate(tiles(width)):
            for copy in copies[half * len(tiles(width)) + j]:
                copy.wait()
            total = total + lax.dot_general(
                factor[:, cols], tokens[:, cols], NT, preferred_element_type=F32
            )
        out[...] = total


def own_products(b, g, a, x):
    rows, width = b.shape
    tokens = x.shape[0]
    return pl.pallas_call(
        own_kernel,
        in_specs=[ANYWHERE] * 4,
        out_specs=[VECTORS] * 4,
        out_shape=[jax.ShapeDtypeStruct((rows, tokens), F32)] * 2
        + [jax.ShapeDtypeStruct((tokens, width), BF16)] * 2,
        scratch_shapes=[pltpu.VMEM(b.shape, BF16)] * 2
        + [pltpu.SemaphoreType.DMA((2, 2, steps_of(width)))],
        compiler_params=params(OWN_LIMIT),
        cost_estimate=cost(4 * rows * tokens * width, 4 * (rows + tokens) * width),
        name="own",
    )(b, g, a, x)


def tiles(width):
    count = steps_of(width)
    return [pl.ds(j * (width // count), width // count) for j in range(count)]


def gate_columns(core, ids, gates, rows, rank):
    total = rows // rank
    row = lax.broadcasted_iota(jnp.int32, (rows, ids.shape[1]), 0)
    adapter = (row // rank + core * (total // 2)) % total
    weight = jnp.zeros((rows, ids.shape[1]), F32)
    for k in range(ids.shape[0]):
        weight = weight + jnp.where(ids[k : k + 1, :] == adapter, gates[k : k + 1, :], 0.0)
    return weight


def store_products(where_ref, at, blocks, lows, outers, send_ref, keep_ref):
    wide = send_ref.shape[1] // blocks
    rows = send_ref.shape[0] // 2
    for j in range(blocks):
        cols = pl.ds(pl.multiple_of(where_ref[at + j] * wide, 128), wide)
        into = pl.ds(j * wide, wide)
        for i, (low, outer) in enumerate(zip(lows, outers)):
            product = jnp.dot(low, outer[:, cols], preferred_element_type=F32).astype(BF16)
            out = pl.ds(i * rows, rows)
            send_ref[out, into] = product[:rows]
            keep_ref[out, into] = product[rows:]


def low_kernel(rank, core_ref, where_ref, ids_ref, gates_ref, grad_ref, act_ref, b_ref, a_ref, g_ref, x_ref,
               lg_ref, la_ref, send_ref, keep_ref):
    rows, width = b_ref.shape
    weight = gate_columns(1 - core_ref[0], ids_ref[...], gates_ref[...], 2 * rows, rank)
    lows = []
    for own, factor, tokens, out in ((grad_ref, b_ref, g_ref, lg_ref), (act_ref, a_ref, x_ref, la_ref)):
        total = jnp.zeros(own.shape, F32)
        for cols in tiles(width):
            total = total + lax.dot_general(
                factor[:, cols], tokens[:, cols], NT, preferred_element_type=F32
            )
        lows.append((jnp.concatenate([total, own[...]], axis=0) * weight).astype(BF16))
        out[...] = lows[-1]
    store_products(where_ref, 0, 1, lows, (x_ref, g_ref), send_ref, keep_ref)


def low_products(core, where, ids, gates, rank, grad, act, b_in, a_in, g, x, wide):
    rows, width = b_in.shape
    tokens = x.shape[0]
    return pl.pallas_call(
        functools.partial(low_kernel, rank),
        in_specs=[SCALARS] * 2 + [VECTORS] * 8,
        out_specs=[VECTORS] * 4,
        out_shape=[jax.ShapeDtypeStruct((2 * rows, tokens), BF16)] * 2
        + [jax.ShapeDtypeStruct((2 * rows, wide), BF16)] * 2,
        compiler_params=params(),
        cost_estimate=cost(4 * rows * tokens * (width + 2 * wide), 4 * (rows + tokens) * width),
        name="low",
    )(core, where, ids, gates, grad, act, b_in, a_in, g, x)


def rest_kernel(blocks, block, where_ref, kept_ref, came_ref, lg_ref, la_ref, x_ref, g_ref, *outs):
    send_ref, keep_ref, outs = outs[0], outs[1], outs[2:]
    near = where_ref[blocks + 1]
    rows = kept_ref.shape[0] * 2 // len(outs)
    for i in range(len(outs) // 2):
        part = pl.ds(i * rows, rows)
        for place, out in ((1 - near, outs[2 * i]), (near, outs[2 * i + 1])):
            cols = pl.ds(pl.multiple_of(place * block, 128), block)
            total = kept_ref[part, cols].astype(F32) + came_ref[part, cols].astype(F32)
            out[...] = total.astype(out.dtype)
    lows = (lg_ref[...], la_ref[...])
    store_products(where_ref, 1, blocks, lows, (x_ref, g_ref), send_ref, keep_ref)


def rest_products(where, kept, came, lg, la, x, g, blocks, block, parts):
    rows = lg.shape[0]
    wide = 2 * blocks * block
    return pl.pallas_call(
        functools.partial(rest_kernel, blocks, block),
        in_specs=[SCALARS] + [VECTORS] * 6,
        out_specs=[VECTORS] * (2 + 2 * parts),
        out_shape=[jax.ShapeDtypeStruct((rows, wide), BF16)] * 2
        + [
            jax.ShapeDtypeStruct((rows // parts, block), BF16),
            jax.ShapeDtypeStruct((rows // parts, block), F32),
        ]
        * parts,
        compiler_params=params(),
        cost_estimate=cost(2 * rows * x.shape[0] * wide, 4 * rows * wide),
        name="rest",
    )(where, kept, came, lg, la, x, g)


def fold_kernel(block, at, where_ref, keep_ref, came_ref, send_ref, own_ref):
    near = where_ref[where_ref.shape[0] - 1]
    for place, out in ((1 - near, send_ref), (near, own_ref)):
        cols = pl.ds(pl.multiple_of((2 * at + place) * block, 128), block)
        out[...] = (keep_ref[:, cols].astype(F32) + came_ref[:, cols].astype(F32)).astype(out.dtype)


def fold(where, block, at, keep, came):
    rows = keep.shape[0]
    return pl.pallas_call(
        functools.partial(fold_kernel, block, at),
        in_specs=[SCALARS] + [VECTORS] * 2,
        out_specs=[VECTORS] * 2,
        out_shape=[
            jax.ShapeDtypeStruct((rows, block), BF16),
            jax.ShapeDtypeStruct((rows, block), F32),
        ],
        compiler_params=params(),
        cost_estimate=cost(2 * rows * block, 14 * rows * block),
        name="fold",
    )(where, keep, came)


def add_kernel(keep_ref, came_ref, out_ref):
    out_ref[...] = (keep_ref[...] + came_ref[...].astype(F32)).astype(out_ref.dtype)


def add(keep, came):
    return pl.pallas_call(
        add_kernel,
        out_shape=jax.ShapeDtypeStruct(keep.shape, BF16),
        compiler_params=params(),
        cost_estimate=cost(keep.size, 8 * keep.size),
        name="add",
    )(keep, came)


def last_kernel(keep_ref, *refs):
    came, (down_ref, up_ref) = refs[:-2], refs[-2:]
    rows = down_ref.shape[0]
    for half, out in ((0, down_ref), (1, up_ref)):
        own = pl.ds(half * rows, rows)
        total = keep_ref[own, :]
        at = 0
        while at < len(came):
            whole = came[at].shape[0] > rows
            total = total + (came[at][own, :] if whole else came[at + half][...]).astype(F32)
            at += 1 if whole else 2
        out[...] = total


def last(keep, came):
    rows, block = keep.shape[0] // 2, keep.shape[1]
    return pl.pallas_call(
        last_kernel,
        in_specs=[VECTORS] * (1 + len(came)),
        out_specs=[VECTORS] * 2,
        out_shape=[jax.ShapeDtypeStruct((rows, block), F32)] * 2,
        compiler_params=params(),
        cost_estimate=cost(keep.size * len(came), keep.size * (8 + 2 * len(came))),
        name="last",
    )(keep, *came)


def input_kernel(low_ref, own_ref, other_ref, out_ref):
    tile = out_ref.shape[1]
    rows = own_ref.shape[0]
    cols = pl.ds(pl.multiple_of(pl.program_id(0) * tile, 128), tile)
    dot = functools.partial(lax.dot_general, dimension_numbers=TN, preferred_element_type=F32)
    out_ref[...] = (
        dot(low_ref[:rows], other_ref[:, cols]) + dot(low_ref[rows:], own_ref[:, cols])
    ).astype(BF16)


def input_gradient(low, own, other):
    tokens = low.shape[1]
    rows, width = own.shape
    steps = steps_of(width)
    tile = width // steps
    return pl.pallas_call(
        input_kernel,
        grid=(steps,),
        in_specs=[VECTORS] * 3,
        out_specs=pl.BlockSpec((tokens, tile), lambda s: (0, s)),
        out_shape=jax.ShapeDtypeStruct((tokens, width), BF16),
        compiler_params=params(),
        cost_estimate=cost(4 * rows * tokens * width, 2 * (2 * rows + tokens) * width),
        name="input",
    )(low, own, other)


def shards(x, g, ids, gates, down_w, up_w):
    tokens, width = x.shape
    count, rank, _ = down_w.shape
    rows = count * rank
    replicas = lax.axis_size("dp")
    block = width // replicas
    core = lax.axis_index("adapter").astype(jnp.int32).reshape(1)
    a = down_w.reshape(rows, width)
    b = up_w.reshape(rows, width)
    ids, gates = ids.T, gates.T
    swap = lambda array: lax.ppermute(array, "adapter", SWAP)
    b_in = swap(b)
    me = lax.axis_index("dp").astype(jnp.int32)
    far, near = me // 2, me % 2
    flip = lambda array, by: lax.ppermute(array, "dp", [(i, i ^ by) for i in range(replicas)])
    steps = replicas // 2
    if steps < 2 or replicas & (replicas - 1) or block % 128:
        return plain(core, ids, gates, rank, x, g, a, b, swap(a), b_in, swap)

    a_in = swap(a)
    grad, act, g_held, x_held = own_products(b, g, a, x)
    order = list(reversed(range(steps)))
    where = jnp.stack([far ^ step for step in order] + [near])
    lg, la, pair, keep = low_products(
        core, where, ids, gates, rank, grad, act, b_in, a_in, g_held, x_held, 2 * block
    )
    rest_pair, rest_keep, *first = rest_products(
        where, keep, swap(pair), lg, la, x_held, g_held, steps - 1, block, 1
    )
    rest_came = swap(rest_pair)
    came = [
        flip(add(own, flip(send, 1)), 2 * order[0]) for send, own in zip(first[::2], first[1::2])
    ]
    for i, step in enumerate(order[1:]):
        send, own = fold(where, block, i, rest_keep, rest_came)
        got = flip(send, 1)
        came.append(flip(add(own, got), 2 * step) if step else got)
    input_grad = input_gradient(lg, a, a_in)
    input_grad, came[-1] = lax.optimization_barrier((input_grad, came[-1]))
    down, up = last(own, came)
    return input_grad, down.reshape(count, rank, block), up.reshape(count, rank, block)


def plain(core, ids, gates, rank, x, g, a, b, a_in, b_in, swap):
    rows = a.shape[0]
    dot = functools.partial(lax.dot_general, preferred_element_type=F32)
    weight = gate_columns(core[0], ids, gates, 2 * rows, rank)
    both_a, both_b = jnp.concatenate([a, a_in]), jnp.concatenate([b, b_in])
    lg = (dot(both_b, g, NT) * weight).astype(BF16)
    la = (dot(both_a, x, NT) * weight).astype(BF16)
    input_grad = dot(lg, both_a, TN).astype(BF16)
    down = jnp.dot(lg, x, preferred_element_type=F32)
    up = jnp.dot(la, g, preferred_element_type=F32)
    own = jnp.concatenate([down[:rows], up[:rows]])
    other = jnp.concatenate([down[rows:], up[rows:]]).astype(BF16)
    total = lax.psum_scatter(
        own + swap(other).astype(F32), "dp", scatter_dimension=1, tiled=True
    ).reshape(2, rows // rank, rank, -1)
    return input_grad, total[0], total[1]


def solution(mesh):
    tok = P(("groups", "dp", "adapter"), None)
    return jax.shard_map(
        shards,
        mesh=mesh,
        in_specs=(tok, tok, tok, tok, P("adapter", None, None), P("adapter", None, None)),
        out_specs=(
            tok,
            P(("groups", "adapter"), None, "dp"),
            P(("groups", "adapter"), None, "dp"),
        ),
        check_vma=False,
    )
```

```python
import functools

import jax
import jax.numpy as jnp
from jax import lax
from jax.experimental import pallas as pl
from jax.experimental.pallas import tpu as pltpu
from jax.sharding import PartitionSpec as P

BF16 = jnp.bfloat16
F32 = jnp.float32
SWAP = [(0, 1), (1, 0)]
VMEM_LIMIT = 12 * 1024 * 1024
OWN_LIMIT = 49 * 1024 * 1024
VECTORS = pl.BlockSpec(memory_space=pltpu.VMEM)
ANYWHERE = pl.BlockSpec(memory_space=pl.ANY)
SCALARS = pl.BlockSpec(memory_space=pltpu.SMEM)
NT = (((1,), (1,)), ((), ()))
TN = (((0,), (0,)), ((), ()))


def params(limit=VMEM_LIMIT):
    return pltpu.CompilerParams(vmem_limit_bytes=limit)


def cost(flops, moved):
    return pl.CostEstimate(flops=int(flops), bytes_accessed=int(moved), transcendentals=0)


def steps_of(width):
    for steps in (4, 7, 2):
        if width % (steps * 128) == 0:
            return steps
    return 1


def own_kernel(b_hbm, g_hbm, x_hbm, grad_ref, g_ref, x_ref, b, sems):
    width = g_ref.shape[1]
    arrays = ((b_hbm, b), (g_hbm, g_ref), (x_hbm, x_ref))
    copies = [
        [
            pltpu.make_async_copy(source.at[:, cols], target.at[:, cols], sems.at[i, j])
            for j, cols in enumerate(tiles(width))
        ]
        for i, (source, target) in enumerate(arrays)
    ]
    for j in range(len(copies[0])):
        copies[0][j].start()
        copies[1][j].start()
    for copy in copies[2]:
        copy.start()
    total = jnp.zeros(grad_ref.shape, F32)
    for j, cols in enumerate(tiles(width)):
        copies[0][j].wait()
        copies[1][j].wait()
        total = total + lax.dot_general(b[:, cols], g_ref[:, cols], NT, preferred_element_type=F32)
    grad_ref[...] = total
    for copy in copies[2]:
        copy.wait()


def own_products(b, g, x):
    rows, width = b.shape
    tokens = x.shape[0]
    return pl.pallas_call(
        own_kernel,
        in_specs=[ANYWHERE] * 3,
        out_specs=[VECTORS] * 3,
        out_shape=[jax.ShapeDtypeStruct((rows, tokens), F32)]
        + [jax.ShapeDtypeStruct((tokens, width), BF16)] * 2,
        scratch_shapes=[pltpu.VMEM(b.shape, BF16), pltpu.SemaphoreType.DMA((3, steps_of(width)))],
        compiler_params=params(OWN_LIMIT),
        cost_estimate=cost(2 * rows * tokens * width, 4 * (rows + tokens) * width),
        name="own",
    )(b, g, x)


def tiles(width):
    count = steps_of(width)
    return [pl.ds(j * (width // count), width // count) for j in range(count)]


def gate_columns(core, ids, gates, rows, rank):
    total = rows // rank
    row = lax.broadcasted_iota(jnp.int32, (rows, ids.shape[1]), 0)
    adapter = (row // rank + core * (total // 2)) % total
    weight = jnp.zeros((rows, ids.shape[1]), F32)
    for k in range(ids.shape[0]):
        weight = weight + jnp.where(ids[k : k + 1, :] == adapter, gates[k : k + 1, :], 0.0)
    return weight


def store_products(where_ref, at, blocks, lows, outers, send_ref, keep_ref):
    wide = send_ref.shape[1] // blocks
    rows = send_ref.shape[0] // 2
    for j in range(blocks):
        cols = pl.ds(pl.multiple_of(where_ref[at + j] * wide, 128), wide)
        into = pl.ds(j * wide, wide)
        for i, (low, outer) in enumerate(zip(lows, outers)):
            product = jnp.dot(low, outer[:, cols], preferred_element_type=F32).astype(BF16)
            out = pl.ds(i * rows, rows)
            send_ref[out, into] = product[:rows]
            keep_ref[out, into] = product[rows:]


def factor_sum(factor, tokens):
    total = jnp.zeros((factor.shape[0], tokens.shape[0]), F32)
    for cols in tiles(factor.shape[1]):
        total = total + lax.dot_general(
            factor[:, cols], tokens[:, cols], NT, preferred_element_type=F32
        )
    return total


def low_kernel(rank, core_ref, where_ref, ids_ref, gates_ref, grad_ref, b_ref, a_ref, a_in_ref, g_ref, x_ref,
               lg_ref, la_ref, send_ref, keep_ref):
    weight = gate_columns(1 - core_ref[0], ids_ref[...], gates_ref[...], 2 * b_ref.shape[0], rank)
    sums = (
        [factor_sum(b_ref, g_ref), grad_ref[...]],
        [factor_sum(a_in_ref, x_ref), factor_sum(a_ref, x_ref)],
    )
    lows = [(jnp.concatenate(pair, axis=0) * weight).astype(BF16) for pair in sums]
    lg_ref[...], la_ref[...] = lows
    store_products(where_ref, 0, 1, lows, (x_ref, g_ref), send_ref, keep_ref)


def low_products(core, where, ids, gates, rank, grad, b_in, a, a_in, g, x, wide):
    rows, width = b_in.shape
    tokens = x.shape[0]
    return pl.pallas_call(
        functools.partial(low_kernel, rank),
        in_specs=[SCALARS] * 2 + [VECTORS] * 8,
        out_specs=[VECTORS] * 4,
        out_shape=[jax.ShapeDtypeStruct((2 * rows, tokens), BF16)] * 2
        + [jax.ShapeDtypeStruct((2 * rows, wide), BF16)] * 2,
        compiler_params=params(),
        cost_estimate=cost(4 * rows * tokens * (width + 2 * wide), 4 * (rows + tokens) * width),
        name="low",
    )(core, where, ids, gates, grad, b_in, a, a_in, g, x)


def rest_kernel(blocks, block, where_ref, kept_ref, came_ref, lg_ref, la_ref, x_ref, g_ref, *outs):
    send_ref, keep_ref, outs = outs[0], outs[1], outs[2:]
    near = where_ref[blocks + 1]
    rows = kept_ref.shape[0] * 2 // len(outs)
    for i in range(len(outs) // 2):
        part = pl.ds(i * rows, rows)
        for place, out in ((1 - near, outs[2 * i]), (near, outs[2 * i + 1])):
            cols = pl.ds(pl.multiple_of(place * block, 128), block)
            total = kept_ref[part, cols].astype(F32) + came_ref[part, cols].astype(F32)
            out[...] = total.astype(out.dtype)
    lows = (lg_ref[...], la_ref[...])
    store_products(where_ref, 1, blocks, lows, (x_ref, g_ref), send_ref, keep_ref)


def rest_products(where, kept, came, lg, la, x, g, blocks, block, parts):
    rows = lg.shape[0]
    wide = 2 * blocks * block
    return pl.pallas_call(
        functools.partial(rest_kernel, blocks, block),
        in_specs=[SCALARS] + [VECTORS] * 6,
        out_specs=[VECTORS] * (2 + 2 * parts),
        out_shape=[jax.ShapeDtypeStruct((rows, wide), BF16)] * 2
        + [
            jax.ShapeDtypeStruct((rows // parts, block), BF16),
            jax.ShapeDtypeStruct((rows // parts, block), F32),
        ]
        * parts,
        compiler_params=params(),
        cost_estimate=cost(2 * rows * x.shape[0] * wide, 4 * rows * wide),
        name="rest",
    )(where, kept, came, lg, la, x, g)


def fold_kernel(block, at, where_ref, keep_ref, came_ref, send_ref, own_ref):
    near = where_ref[where_ref.shape[0] - 1]
    for place, out in ((1 - near, send_ref), (near, own_ref)):
        cols = pl.ds(pl.multiple_of((2 * at + place) * block, 128), block)
        out[...] = (keep_ref[:, cols].astype(F32) + came_ref[:, cols].astype(F32)).astype(out.dtype)


def fold(where, block, at, keep, came):
    rows = keep.shape[0]
    return pl.pallas_call(
        functools.partial(fold_kernel, block, at),
        in_specs=[SCALARS] + [VECTORS] * 2,
        out_specs=[VECTORS] * 2,
        out_shape=[
            jax.ShapeDtypeStruct((rows, block), BF16),
            jax.ShapeDtypeStruct((rows, block), F32),
        ],
        compiler_params=params(),
        cost_estimate=cost(2 * rows * block, 14 * rows * block),
        name="fold",
    )(where, keep, came)


def add_kernel(keep_ref, came_ref, out_ref):
    out_ref[...] = (keep_ref[...] + came_ref[...].astype(F32)).astype(out_ref.dtype)


def add(keep, came):
    return pl.pallas_call(
        add_kernel,
        out_shape=jax.ShapeDtypeStruct(keep.shape, BF16),
        compiler_params=params(),
        cost_estimate=cost(keep.size, 8 * keep.size),
        name="add",
    )(keep, came)


def total_kernel(keep_ref, *refs):
    total = keep_ref[...]
    for ref in refs[:-1]:
        total = total + ref[...].astype(F32)
    refs[-1][...] = total


def total(keep, came):
    return pl.pallas_call(
        total_kernel,
        in_specs=[VECTORS] * (1 + len(came)),
        out_specs=VECTORS,
        out_shape=jax.ShapeDtypeStruct(keep.shape, F32),
        compiler_params=params(),
        cost_estimate=cost(keep.size * len(came), keep.size * (8 + 2 * len(came))),
        name="total",
    )(keep, *came)


def last_kernel(total_ref, came_ref, down_ref, up_ref):
    rows = down_ref.shape[0]
    down_ref[...] = total_ref[:rows] + came_ref[:rows].astype(F32)
    up_ref[...] = total_ref[rows:] + came_ref[rows:].astype(F32)


def last(total, came):
    rows, block = total.shape[0] // 2, total.shape[1]
    return pl.pallas_call(
        last_kernel,
        in_specs=[VECTORS] * 2,
        out_specs=[VECTORS] * 2,
        out_shape=[jax.ShapeDtypeStruct((rows, block), F32)] * 2,
        compiler_params=params(),
        cost_estimate=cost(came.size, 10 * came.size),
        name="last",
    )(total, came)


def input_kernel(low_ref, own_ref, other_ref, out_ref):
    tile = out_ref.shape[1]
    rows = own_ref.shape[0]
    cols = pl.ds(pl.multiple_of(pl.program_id(0) * tile, 128), tile)
    dot = functools.partial(lax.dot_general, dimension_numbers=TN, preferred_element_type=F32)
    out_ref[...] = (
        dot(low_ref[:rows], other_ref[:, cols]) + dot(low_ref[rows:], own_ref[:, cols])
    ).astype(BF16)


def input_gradient(low, own, other):
    tokens = low.shape[1]
    rows, width = own.shape
    steps = steps_of(width)
    tile = width // steps
    return pl.pallas_call(
        input_kernel,
        grid=(steps,),
        in_specs=[VECTORS] * 3,
        out_specs=pl.BlockSpec((tokens, tile), lambda s: (0, s)),
        out_shape=jax.ShapeDtypeStruct((tokens, width), BF16),
        compiler_params=params(),
        cost_estimate=cost(4 * rows * tokens * width, 2 * (2 * rows + tokens) * width),
        name="input",
    )(low, own, other)


def shards(x, g, ids, gates, down_w, up_w):
    tokens, width = x.shape
    count, rank, _ = down_w.shape
    rows = count * rank
    replicas = lax.axis_size("dp")
    block = width // replicas
    core = lax.axis_index("adapter").astype(jnp.int32).reshape(1)
    a = down_w.reshape(rows, width)
    b = up_w.reshape(rows, width)
    ids, gates = ids.T, gates.T
    swap = lambda array: lax.ppermute(array, "adapter", SWAP)
    b_in = swap(b)
    me = lax.axis_index("dp").astype(jnp.int32)
    far, near = me // 2, me % 2
    flip = lambda array, by: lax.ppermute(array, "dp", [(i, i ^ by) for i in range(replicas)])
    steps = replicas // 2
    if steps < 2 or replicas & (replicas - 1) or block % 128:
        return plain(core, ids, gates, rank, x, g, a, b, swap(a), b_in, swap)

    a_in = swap(a)
    grad, g_held, x_held = own_products(b, g, x)
    order = list(reversed(range(steps)))
    where = jnp.stack([far ^ step for step in order] + [near])
    lg, la, pair, keep = low_products(
        core, where, ids, gates, rank, grad, b_in, a, a_in, g_held, x_held, 2 * block
    )
    rest_pair, rest_keep, *first = rest_products(
        where, keep, swap(pair), lg, la, x_held, g_held, steps - 1, block, 1
    )
    rest_came = swap(rest_pair)
    send, own = first
    came = []
    for i, step in enumerate(order):
        if i:
            send, own = fold(where, block, i - 1, rest_keep, rest_came)
        got = flip(send, 1)
        if step == 0:
            came.append(got)
        elif step == 1:
            nearest = flip(add(own, got), 2)
        else:
            came.append(flip(add(own, got), 2 * step))
    input_grad = input_gradient(lg, a, a_in)
    input_grad, came[-1] = lax.optimization_barrier((input_grad, came[-1]))
    down, up = last(total(own, came), nearest)
    return input_grad, down.reshape(count, rank, block), up.reshape(count, rank, block)


def plain(core, ids, gates, rank, x, g, a, b, a_in, b_in, swap):
    rows = a.shape[0]
    dot = functools.partial(lax.dot_general, preferred_element_type=F32)
    weight = gate_columns(core[0], ids, gates, 2 * rows, rank)
    both_a, both_b = jnp.concatenate([a, a_in]), jnp.concatenate([b, b_in])
    lg = (dot(both_b, g, NT) * weight).astype(BF16)
    la = (dot(both_a, x, NT) * weight).astype(BF16)
    input_grad = dot(lg, both_a, TN).astype(BF16)
    down = jnp.dot(lg, x, preferred_element_type=F32)
    up = jnp.dot(la, g, preferred_element_type=F32)
    own = jnp.concatenate([down[:rows], up[:rows]])
    other = jnp.concatenate([down[rows:], up[rows:]]).astype(BF16)
    total = lax.psum_scatter(
        own + swap(other).astype(F32), "dp", scatter_dimension=1, tiled=True
    ).reshape(2, rows // rank, rank, -1)
    return input_grad, total[0], total[1]


def solution(mesh):
    tok = P(("groups", "dp", "adapter"), None)
    return jax.shard_map(
        shards,
        mesh=mesh,
        in_specs=(tok, tok, tok, tok, P("adapter", None, None), P("adapter", None, None)),
        out_specs=(
            tok,
            P(("groups", "adapter"), None, "dp"),
            P(("groups", "adapter"), None, "dp"),
        ),
        check_vma=False,
    )
```

```python
import functools

import jax
import jax.numpy as jnp
from jax import lax
from jax.experimental import pallas as pl
from jax.experimental.pallas import tpu as pltpu
from jax.sharding import PartitionSpec as P

BF16 = jnp.bfloat16
F32 = jnp.float32
SWAP = [(0, 1), (1, 0)]
VMEM_LIMIT = 12 * 1024 * 1024
OWN_LIMIT = 49 * 1024 * 1024
VECTORS = pl.BlockSpec(memory_space=pltpu.VMEM)
ANYWHERE = pl.BlockSpec(memory_space=pl.ANY)
SCALARS = pl.BlockSpec(memory_space=pltpu.SMEM)
NT = (((1,), (1,)), ((), ()))
TN = (((0,), (0,)), ((), ()))


def params(limit=VMEM_LIMIT):
    return pltpu.CompilerParams(vmem_limit_bytes=limit)


def cost(flops, moved):
    return pl.CostEstimate(flops=int(flops), bytes_accessed=int(moved), transcendentals=0)


def steps_of(width):
    for steps in (4, 7, 2):
        if width % (steps * 128) == 0:
            return steps
    return 1


def own_kernel(b_hbm, g_hbm, x_hbm, grad_ref, g_ref, x_ref, b, sems):
    width = g_ref.shape[1]
    arrays = ((b_hbm, b), (g_hbm, g_ref), (x_hbm, x_ref))
    copies = [
        [
            pltpu.make_async_copy(source.at[:, cols], target.at[:, cols], sems.at[i, j])
            for j, cols in enumerate(tiles(width))
        ]
        for i, (source, target) in enumerate(arrays)
    ]
    for j in range(len(copies[0])):
        copies[0][j].start()
        copies[1][j].start()
    for copy in copies[2]:
        copy.start()
    total = jnp.zeros(grad_ref.shape, F32)
    for j, cols in enumerate(tiles(width)):
        copies[0][j].wait()
        copies[1][j].wait()
        total = total + lax.dot_general(b[:, cols], g_ref[:, cols], NT, preferred_element_type=F32)
    grad_ref[...] = total
    for copy in copies[2]:
        copy.wait()


def own_products(b, g, x):
    rows, width = b.shape
    tokens = x.shape[0]
    return pl.pallas_call(
        own_kernel,
        in_specs=[ANYWHERE] * 3,
        out_specs=[VECTORS] * 3,
        out_shape=[jax.ShapeDtypeStruct((rows, tokens), F32)]
        + [jax.ShapeDtypeStruct((tokens, width), BF16)] * 2,
        scratch_shapes=[pltpu.VMEM(b.shape, BF16), pltpu.SemaphoreType.DMA((3, steps_of(width)))],
        compiler_params=params(OWN_LIMIT),
        cost_estimate=cost(2 * rows * tokens * width, 4 * (rows + tokens) * width),
        name="own",
    )(b, g, x)


def tiles(width):
    count = steps_of(width)
    return [pl.ds(j * (width // count), width // count) for j in range(count)]


def gate_columns(core, ids, gates, rows, rank):
    total = rows // rank
    row = lax.broadcasted_iota(jnp.int32, (rows, ids.shape[1]), 0)
    adapter = (row // rank + core * (total // 2)) % total
    weight = jnp.zeros((rows, ids.shape[1]), F32)
    for k in range(ids.shape[0]):
        weight = weight + jnp.where(ids[k : k + 1, :] == adapter, gates[k : k + 1, :], 0.0)
    return weight


def store_products(where_ref, at, blocks, lows, outers, send_ref, keep_ref):
    wide = send_ref.shape[1] // blocks
    rows = send_ref.shape[0] // 2
    for j in range(blocks):
        cols = pl.ds(pl.multiple_of(where_ref[at + j] * wide, 128), wide)
        into = pl.ds(j * wide, wide)
        for i, (low, outer) in enumerate(zip(lows, outers)):
            product = jnp.dot(low, outer[:, cols], preferred_element_type=F32).astype(BF16)
            out = pl.ds(i * rows, rows)
            send_ref[out, into] = product[:rows]
            keep_ref[out, into] = product[rows:]


def factor_sum(factor, tokens):
    total = jnp.zeros((factor.shape[0], tokens.shape[0]), F32)
    for cols in tiles(factor.shape[1]):
        total = total + lax.dot_general(
            factor[:, cols], tokens[:, cols], NT, preferred_element_type=F32
        )
    return total


def low_kernel(rank, core_ref, where_ref, ids_ref, gates_ref, grad_ref, b_ref, a_ref, a_in_ref, g_ref, x_ref,
               lg_ref, la_ref, send_ref, keep_ref):
    weight = gate_columns(1 - core_ref[0], ids_ref[...], gates_ref[...], 2 * b_ref.shape[0], rank)
    sums = (
        [factor_sum(b_ref, g_ref), grad_ref[...]],
        [factor_sum(a_in_ref, x_ref), factor_sum(a_ref, x_ref)],
    )
    lows = [(jnp.concatenate(pair, axis=0) * weight).astype(BF16) for pair in sums]
    lg_ref[...], la_ref[...] = lows
    store_products(where_ref, 0, 1, lows, (x_ref, g_ref), send_ref, keep_ref)


def low_products(core, where, ids, gates, rank, grad, b_in, a, a_in, g, x, wide):
    rows, width = b_in.shape
    tokens = x.shape[0]
    return pl.pallas_call(
        functools.partial(low_kernel, rank),
        in_specs=[SCALARS] * 2 + [VECTORS] * 8,
        out_specs=[VECTORS] * 4,
        out_shape=[jax.ShapeDtypeStruct((2 * rows, tokens), BF16)] * 2
        + [jax.ShapeDtypeStruct((2 * rows, wide), BF16)] * 2,
        compiler_params=params(),
        cost_estimate=cost(4 * rows * tokens * (width + 2 * wide), 4 * (rows + tokens) * width),
        name="low",
    )(core, where, ids, gates, grad, b_in, a, a_in, g, x)


def rest_kernel(blocks, block, where_ref, kept_ref, came_ref, lg_ref, la_ref, x_ref, g_ref, *outs):
    send_ref, keep_ref, outs = outs[0], outs[1], outs[2:]
    near = where_ref[blocks + 1]
    rows = kept_ref.shape[0] * 2 // len(outs)
    for i in range(len(outs) // 2):
        part = pl.ds(i * rows, rows)
        for place, out in ((1 - near, outs[2 * i]), (near, outs[2 * i + 1])):
            cols = pl.ds(pl.multiple_of(place * block, 128), block)
            total = kept_ref[part, cols].astype(F32) + came_ref[part, cols].astype(F32)
            out[...] = total.astype(out.dtype)
    lows = (lg_ref[...], la_ref[...])
    store_products(where_ref, 1, blocks, lows, (x_ref, g_ref), send_ref, keep_ref)


def rest_products(where, kept, came, lg, la, x, g, blocks, block, parts):
    rows = lg.shape[0]
    wide = 2 * blocks * block
    return pl.pallas_call(
        functools.partial(rest_kernel, blocks, block),
        in_specs=[SCALARS] + [VECTORS] * 6,
        out_specs=[VECTORS] * (2 + 2 * parts),
        out_shape=[jax.ShapeDtypeStruct((rows, wide), BF16)] * 2
        + [
            jax.ShapeDtypeStruct((rows // parts, block), BF16),
            jax.ShapeDtypeStruct((rows // parts, block), F32),
        ]
        * parts,
        compiler_params=params(),
        cost_estimate=cost(2 * rows * x.shape[0] * wide, 4 * rows * wide),
        name="rest",
    )(where, kept, came, lg, la, x, g)


def fold_kernel(block, at, where_ref, keep_ref, came_ref, send_ref, own_ref):
    near = where_ref[where_ref.shape[0] - 1]
    for place, out in ((1 - near, send_ref), (near, own_ref)):
        cols = pl.ds(pl.multiple_of((2 * at + place) * block, 128), block)
        out[...] = (keep_ref[:, cols].astype(F32) + came_ref[:, cols].astype(F32)).astype(out.dtype)


def fold(where, block, at, keep, came):
    rows = keep.shape[0]
    return pl.pallas_call(
        functools.partial(fold_kernel, block, at),
        in_specs=[SCALARS] + [VECTORS] * 2,
        out_specs=[VECTORS] * 2,
        out_shape=[
            jax.ShapeDtypeStruct((rows, block), BF16),
            jax.ShapeDtypeStruct((rows, block), F32),
        ],
        compiler_params=params(),
        cost_estimate=cost(2 * rows * block, 14 * rows * block),
        name="fold",
    )(where, keep, came)


def add_kernel(keep_ref, *refs):
    came, out_ref = refs[:-1], refs[-1]
    total = keep_ref[...]
    for ref in came:
        total = total + ref[...].astype(F32)
    out_ref[...] = total.astype(out_ref.dtype)


def add(keep, *came):
    return pl.pallas_call(
        add_kernel,
        in_specs=[VECTORS] * (1 + len(came)),
        out_specs=VECTORS,
        out_shape=jax.ShapeDtypeStruct(keep.shape, BF16),
        compiler_params=params(),
        cost_estimate=cost(keep.size, 8 * keep.size),
        name="add",
    )(keep, *came)


def halves_kernel(keep_ref, came_ref, *outs):
    rows = outs[0].shape[0]
    for half, out in enumerate(outs):
        part = pl.ds(half * rows, rows)
        out[...] = (keep_ref[part, :] + came_ref[part, :].astype(F32)).astype(out.dtype)


def add_halves(keep, came, dtypes):
    rows, block = keep.shape[0] // 2, keep.shape[1]
    return pl.pallas_call(
        halves_kernel,
        in_specs=[VECTORS] * 2,
        out_specs=[VECTORS] * 2,
        out_shape=[jax.ShapeDtypeStruct((rows, block), dtype) for dtype in dtypes],
        compiler_params=params(),
        cost_estimate=cost(keep.size, 9 * keep.size),
        name="halves",
    )(keep, came)


def total_kernel(both, downs, keep_ref, *refs):
    came, outs = refs[: len(refs) - 2], refs[len(refs) - 2 :]
    rows = outs[0].shape[0]
    for half, out in enumerate(outs):
        part = pl.ds(half * rows, rows)
        total = keep_ref[part, :]
        for ref in came[:both]:
            total = total + ref[part, :].astype(F32)
        for ref in came[both:][slice(downs) if half == 0 else slice(downs, None)]:
            total = total + ref[...].astype(F32)
        out[...] = total


def total(keep, both, downs, ups):
    rows, block = keep.shape[0] // 2, keep.shape[1]
    came = [*both, *downs, *ups]
    return pl.pallas_call(
        functools.partial(total_kernel, len(both), len(downs)),
        in_specs=[VECTORS] * (1 + len(came)),
        out_specs=[VECTORS] * 2,
        out_shape=[jax.ShapeDtypeStruct((rows, block), F32)] * 2,
        compiler_params=params(),
        cost_estimate=cost(keep.size * len(came), keep.size * (8 + 2 * len(came))),
        name="total",
    )(keep, *came)


def last_kernel(down_in, up_in, down_came, up_came, down_ref, up_ref):
    down_ref[...] = down_in[...] + down_came[...].astype(F32)
    up_ref[...] = up_in[...] + up_came[...].astype(F32)


def last(down, up, down_came, up_came):
    return pl.pallas_call(
        last_kernel,
        in_specs=[VECTORS] * 4,
        out_specs=[VECTORS] * 2,
        out_shape=[jax.ShapeDtypeStruct(down.shape, F32)] * 2,
        compiler_params=params(),
        cost_estimate=cost(down.size, 10 * down.size),
        name="last",
    )(down, up, down_came, up_came)


def input_kernel(low_ref, own_ref, other_ref, out_ref):
    tile = out_ref.shape[1]
    rows = own_ref.shape[0]
    cols = pl.ds(pl.multiple_of(pl.program_id(0) * tile, 128), tile)
    dot = functools.partial(lax.dot_general, dimension_numbers=TN, preferred_element_type=F32)
    out_ref[...] = (
        dot(low_ref[:rows], other_ref[:, cols]) + dot(low_ref[rows:], own_ref[:, cols])
    ).astype(BF16)


def input_gradient(low, own, other):
    tokens = low.shape[1]
    rows, width = own.shape
    steps = steps_of(width)
    tile = width // steps
    return pl.pallas_call(
        input_kernel,
        grid=(steps,),
        in_specs=[VECTORS] * 3,
        out_specs=pl.BlockSpec((tokens, tile), lambda s: (0, s)),
        out_shape=jax.ShapeDtypeStruct((tokens, width), BF16),
        compiler_params=params(),
        cost_estimate=cost(4 * rows * tokens * width, 2 * (2 * rows + tokens) * width),
        name="input",
    )(low, own, other)


def shards(x, g, ids, gates, down_w, up_w):
    tokens, width = x.shape
    count, rank, _ = down_w.shape
    rows = count * rank
    replicas = lax.axis_size("dp")
    block = width // replicas
    core = lax.axis_index("adapter").astype(jnp.int32).reshape(1)
    a = down_w.reshape(rows, width)
    b = up_w.reshape(rows, width)
    ids, gates = ids.T, gates.T
    swap = lambda array: lax.ppermute(array, "adapter", SWAP)
    b_in = swap(b)
    me = lax.axis_index("dp").astype(jnp.int32)
    far, near = me // 2, me % 2
    flip = lambda array, by: lax.ppermute(array, "dp", [(i, i ^ by) for i in range(replicas)])
    steps = replicas // 2
    if steps < 2 or replicas & (replicas - 1) or block % 128:
        return plain(core, ids, gates, rank, x, g, a, b, swap(a), b_in, swap)

    a_in = swap(a)
    grad, g_held, x_held = own_products(b, g, x)
    order = list(reversed(range(steps)))
    where = jnp.stack([far ^ step for step in order] + [near])
    lg, la, pair, keep = low_products(
        core, where, ids, gates, rank, grad, b_in, a, a_in, g_held, x_held, 2 * block
    )
    rest_pair, rest_keep, *first = rest_products(
        where, keep, swap(pair), lg, la, x_held, g_held, steps - 1, block, 1
    )
    rest_came = swap(rest_pair)
    send, own = first
    both, downs, ups = [], [], []
    for i, step in enumerate(order):
        if i:
            send, own = fold(where, block, i - 1, rest_keep, rest_came)
        got = flip(send, 1)
        if step == 0:
            both.append(got)
        elif step == 1:
            nearest = [flip(half, 2) for half in add_halves(own, got, (BF16, BF16))]
        elif steps != 4:
            both.append(flip(add(own, got), 2 * step))
        elif step == 3:
            passed = [flip(half, 2) for half in add_halves(own, got, (BF16, BF16))]
        else:
            mine = add_halves(own, got, (F32, F32))
            for half, came, into in zip(mine, passed, (downs, ups)):
                into.append(flip(add(half, came), 4))
    input_grad = input_gradient(lg, a, a_in)
    input_grad, both[-1] = lax.optimization_barrier((input_grad, both[-1]))
    down, up = last(*total(own, both, downs, ups), *nearest)
    return input_grad, down.reshape(count, rank, block), up.reshape(count, rank, block)


def plain(core, ids, gates, rank, x, g, a, b, a_in, b_in, swap):
    rows = a.shape[0]
    dot = functools.partial(lax.dot_general, preferred_element_type=F32)
    weight = gate_columns(core[0], ids, gates, 2 * rows, rank)
    both_a, both_b = jnp.concatenate([a, a_in]), jnp.concatenate([b, b_in])
    lg = (dot(both_b, g, NT) * weight).astype(BF16)
    la = (dot(both_a, x, NT) * weight).astype(BF16)
    input_grad = dot(lg, both_a, TN).astype(BF16)
    down = jnp.dot(lg, x, preferred_element_type=F32)
    up = jnp.dot(la, g, preferred_element_type=F32)
    own = jnp.concatenate([down[:rows], up[:rows]])
    other = jnp.concatenate([down[rows:], up[rows:]]).astype(BF16)
    total = lax.psum_scatter(
        own + swap(other).astype(F32), "dp", scatter_dimension=1, tiled=True
    ).reshape(2, rows // rank, rank, -1)
    return input_grad, total[0], total[1]


def solution(mesh):
    tok = P(("groups", "dp", "adapter"), None)
    return jax.shard_map(
        shards,
        mesh=mesh,
        in_specs=(tok, tok, tok, tok, P("adapter", None, None), P("adapter", None, None)),
        out_specs=(
            tok,
            P(("groups", "adapter"), None, "dp"),
            P(("groups", "adapter"), None, "dp"),
        ),
        check_vma=False,
    )
```

```python
import functools

import jax
import jax.numpy as jnp
from jax import lax
from jax.experimental import pallas as pl
from jax.experimental.pallas import tpu as pltpu
from jax.sharding import PartitionSpec as P

BF16 = jnp.bfloat16
F32 = jnp.float32
SWAP = [(0, 1), (1, 0)]
VMEM_LIMIT = 12 * 1024 * 1024
HOLD_LIMIT = 50 * 1024 * 1024
VECTORS = pl.BlockSpec(memory_space=pltpu.VMEM)
ANYWHERE = pl.BlockSpec(memory_space=pl.ANY)
SCALARS = pl.BlockSpec(memory_space=pltpu.SMEM)
NT = (((1,), (1,)), ((), ()))
TN = (((0,), (0,)), ((), ()))


def params(limit=VMEM_LIMIT):
    return pltpu.CompilerParams(vmem_limit_bytes=limit)


def cost(flops, moved):
    return pl.CostEstimate(flops=int(flops), bytes_accessed=int(moved), transcendentals=0)


def steps_of(width):
    for steps in (4, 7, 2):
        if width % (steps * 128) == 0:
            return steps
    return 1


def hold_kernel(g_hbm, x_hbm, g_ref, x_ref, sems):
    copies = [
        pltpu.make_async_copy(source.at[:, cols], target.at[:, cols], sems.at[i, j])
        for i, (source, target) in enumerate(((g_hbm, g_ref), (x_hbm, x_ref)))
        for j, cols in enumerate(tiles(g_ref.shape[1]))
    ]
    for copy in copies:
        copy.start()
    for copy in copies:
        copy.wait()


def hold(g, x):
    return pl.pallas_call(
        hold_kernel,
        in_specs=[ANYWHERE] * 2,
        out_specs=[VECTORS] * 2,
        out_shape=[jax.ShapeDtypeStruct(x.shape, BF16)] * 2,
        scratch_shapes=[pltpu.SemaphoreType.DMA((2, steps_of(x.shape[1])))],
        compiler_params=params(HOLD_LIMIT),
        cost_estimate=cost(128 * x.size, 8 * x.size),
        name="hold",
    )(g, x)


def tiles(width):
    count = steps_of(width)
    return [pl.ds(j * (width // count), width // count) for j in range(count)]


def gate_columns(core, ids, gates, rows, rank):
    total = rows // rank
    row = lax.broadcasted_iota(jnp.int32, (rows, ids.shape[1]), 0)
    adapter = (row // rank + core * (total // 2)) % total
    weight = jnp.zeros((rows, ids.shape[1]), F32)
    for k in range(ids.shape[0]):
        weight = weight + jnp.where(ids[k : k + 1, :] == adapter, gates[k : k + 1, :], 0.0)
    return weight


def store_products(where_ref, at, blocks, lows, outers, send_ref, keep_ref):
    wide = send_ref.shape[1] // blocks
    rows = send_ref.shape[0] // 2
    for j in range(blocks):
        cols = pl.ds(pl.multiple_of(where_ref[at + j] * wide, 128), wide)
        into = pl.ds(j * wide, wide)
        for i, (low, outer) in enumerate(zip(lows, outers)):
            product = jnp.dot(low, outer[:, cols], preferred_element_type=F32).astype(BF16)
            out = pl.ds(i * rows, rows)
            send_ref[out, into] = product[:rows]
            keep_ref[out, into] = product[rows:]


def factor_sum(tokens, *factors):
    total = 0.0
    for cols in tiles(tokens.shape[1]):
        rows = jnp.concatenate([factor[:, cols] for factor in factors], axis=0)
        total = total + lax.dot_general(rows, tokens[:, cols], NT, preferred_element_type=F32)
    return total


def low_kernel(rank, core_ref, where_ref, ids_ref, gates_ref, b_ref, b_in_ref, a_ref, a_in_ref, g_ref, x_ref,
               lg_ref, la_ref, send_ref, keep_ref):
    weight = gate_columns(1 - core_ref[0], ids_ref[...], gates_ref[...], 2 * b_ref.shape[0], rank)
    sums = factor_sum(g_ref, b_in_ref, b_ref), factor_sum(x_ref, a_in_ref, a_ref)
    lows = [(rows * weight).astype(BF16) for rows in sums]
    lg_ref[...], la_ref[...] = lows
    store_products(where_ref, 0, 1, lows, (x_ref, g_ref), send_ref, keep_ref)


def low_products(core, where, ids, gates, rank, b, b_in, a, a_in, g, x, wide):
    rows, width = b_in.shape
    tokens = x.shape[0]
    return pl.pallas_call(
        functools.partial(low_kernel, rank),
        in_specs=[SCALARS] * 2 + [VECTORS] * 8,
        out_specs=[VECTORS] * 4,
        out_shape=[jax.ShapeDtypeStruct((2 * rows, tokens), BF16)] * 2
        + [jax.ShapeDtypeStruct((2 * rows, wide), BF16)] * 2,
        compiler_params=params(),
        cost_estimate=cost(4 * rows * tokens * (width + 2 * wide), 4 * (rows + tokens) * width),
        name="low",
    )(core, where, ids, gates, b, b_in, a, a_in, g, x)


def rest_kernel(blocks, block, where_ref, kept_ref, came_ref, lg_ref, la_ref, x_ref, g_ref, *outs):
    send_ref, keep_ref, outs = outs[0], outs[1], outs[2:]
    near = where_ref[blocks + 1]
    rows = kept_ref.shape[0] * 2 // len(outs)
    for i in range(len(outs) // 2):
        part = pl.ds(i * rows, rows)
        for place, out in ((1 - near, outs[2 * i]), (near, outs[2 * i + 1])):
            cols = pl.ds(pl.multiple_of(place * block, 128), block)
            total = kept_ref[part, cols].astype(F32) + came_ref[part, cols].astype(F32)
            out[...] = total.astype(out.dtype)
    lows = (lg_ref[...], la_ref[...])
    store_products(where_ref, 1, blocks, lows, (x_ref, g_ref), send_ref, keep_ref)


def rest_products(where, kept, came, lg, la, x, g, blocks, block, parts):
    rows = lg.shape[0]
    wide = 2 * blocks * block
    return pl.pallas_call(
        functools.partial(rest_kernel, blocks, block),
        in_specs=[SCALARS] + [VECTORS] * 6,
        out_specs=[VECTORS] * (2 + 2 * parts),
        out_shape=[jax.ShapeDtypeStruct((rows, wide), BF16)] * 2
        + [
            jax.ShapeDtypeStruct((rows // parts, block), BF16),
            jax.ShapeDtypeStruct((rows // parts, block), F32),
        ]
        * parts,
        compiler_params=params(),
        cost_estimate=cost(2 * rows * x.shape[0] * wide, 4 * rows * wide),
        name="rest",
    )(where, kept, came, lg, la, x, g)


def fold_kernel(block, at, where_ref, keep_ref, came_ref, send_ref, own_ref):
    near = where_ref[where_ref.shape[0] - 1]
    for place, out in ((1 - near, send_ref), (near, own_ref)):
        cols = pl.ds(pl.multiple_of((2 * at + place) * block, 128), block)
        out[...] = (keep_ref[:, cols].astype(F32) + came_ref[:, cols].astype(F32)).astype(out.dtype)


def fold(where, block, at, keep, came):
    rows = keep.shape[0]
    return pl.pallas_call(
        functools.partial(fold_kernel, block, at),
        in_specs=[SCALARS] + [VECTORS] * 2,
        out_specs=[VECTORS] * 2,
        out_shape=[
            jax.ShapeDtypeStruct((rows, block), BF16),
            jax.ShapeDtypeStruct((rows, block), F32),
        ],
        compiler_params=params(),
        cost_estimate=cost(2 * rows * block, 14 * rows * block),
        name="fold",
    )(where, keep, came)


def add_kernel(keep_ref, *refs):
    came, out_ref = refs[:-1], refs[-1]
    total = keep_ref[...]
    for ref in came:
        total = total + ref[...].astype(F32)
    out_ref[...] = total.astype(out_ref.dtype)


def add(keep, *came):
    return pl.pallas_call(
        add_kernel,
        in_specs=[VECTORS] * (1 + len(came)),
        out_specs=VECTORS,
        out_shape=jax.ShapeDtypeStruct(keep.shape, BF16),
        compiler_params=params(),
        cost_estimate=cost(keep.size, 8 * keep.size),
        name="add",
    )(keep, *came)


def halves_kernel(keep_ref, came_ref, *outs):
    rows = outs[0].shape[0]
    for half, out in enumerate(outs):
        part = pl.ds(half * rows, rows)
        out[...] = (keep_ref[part, :] + came_ref[part, :].astype(F32)).astype(out.dtype)


def add_halves(keep, came, dtypes):
    rows, block = keep.shape[0] // 2, keep.shape[1]
    return pl.pallas_call(
        halves_kernel,
        in_specs=[VECTORS] * 2,
        out_specs=[VECTORS] * 2,
        out_shape=[jax.ShapeDtypeStruct((rows, block), dtype) for dtype in dtypes],
        compiler_params=params(),
        cost_estimate=cost(keep.size, 9 * keep.size),
        name="halves",
    )(keep, came)


def total_kernel(both, downs, keep_ref, *refs):
    came, outs = refs[: len(refs) - 2], refs[len(refs) - 2 :]
    rows = outs[0].shape[0]
    for half, out in enumerate(outs):
        part = pl.ds(half * rows, rows)
        total = keep_ref[part, :]
        for ref in came[:both]:
            total = total + ref[part, :].astype(F32)
        for ref in came[both:][slice(downs) if half == 0 else slice(downs, None)]:
            total = total + ref[...].astype(F32)
        out[...] = total


def total(keep, both, downs, ups):
    rows, block = keep.shape[0] // 2, keep.shape[1]
    came = [*both, *downs, *ups]
    return pl.pallas_call(
        functools.partial(total_kernel, len(both), len(downs)),
        in_specs=[VECTORS] * (1 + len(came)),
        out_specs=[VECTORS] * 2,
        out_shape=[jax.ShapeDtypeStruct((rows, block), F32)] * 2,
        compiler_params=params(),
        cost_estimate=cost(keep.size * len(came), keep.size * (8 + 2 * len(came))),
        name="total",
    )(keep, *came)


def last_kernel(total_ref, came_ref, out_ref):
    out_ref[...] = total_ref[...] + came_ref[...].astype(F32)


def last(total, came):
    return pl.pallas_call(
        last_kernel,
        in_specs=[VECTORS] * 2,
        out_specs=VECTORS,
        out_shape=jax.ShapeDtypeStruct(total.shape, F32),
        compiler_params=params(),
        cost_estimate=cost(total.size, 10 * total.size),
        name="last",
    )(total, came)


def input_kernel(low_ref, own_ref, other_ref, out_ref):
    tile = out_ref.shape[1]
    rows = own_ref.shape[0]
    cols = pl.ds(pl.multiple_of(pl.program_id(0) * tile, 128), tile)
    dot = functools.partial(lax.dot_general, dimension_numbers=TN, preferred_element_type=F32)
    out_ref[...] = (
        dot(low_ref[:rows], other_ref[:, cols]) + dot(low_ref[rows:], own_ref[:, cols])
    ).astype(BF16)


def input_gradient(low, own, other):
    tokens = low.shape[1]
    rows, width = own.shape
    steps = steps_of(width)
    tile = width // steps
    return pl.pallas_call(
        input_kernel,
        grid=(steps,),
        in_specs=[VECTORS] * 3,
        out_specs=pl.BlockSpec((tokens, tile), lambda s: (0, s)),
        out_shape=jax.ShapeDtypeStruct((tokens, width), BF16),
        compiler_params=params(),
        cost_estimate=cost(4 * rows * tokens * width, 2 * (2 * rows + tokens) * width),
        name="input",
    )(low, own, other)


def shards(x, g, ids, gates, down_w, up_w):
    tokens, width = x.shape
    count, rank, _ = down_w.shape
    rows = count * rank
    replicas = lax.axis_size("dp")
    block = width // replicas
    core = lax.axis_index("adapter").astype(jnp.int32).reshape(1)
    a = down_w.reshape(rows, width)
    b = up_w.reshape(rows, width)
    ids, gates = ids.T, gates.T
    swap = lambda array: lax.ppermute(array, "adapter", SWAP)
    b_in = swap(b)
    me = lax.axis_index("dp").astype(jnp.int32)
    far, near = me // 2, me % 2
    flip = lambda array, by: lax.ppermute(array, "dp", [(i, i ^ by) for i in range(replicas)])
    steps = replicas // 2
    if steps < 2 or replicas & (replicas - 1) or block % 128:
        return plain(core, ids, gates, rank, x, g, a, b, swap(a), b_in, swap)

    a_in = swap(a)
    g_held, x_held = hold(g, x)
    order = list(reversed(range(steps)))
    where = jnp.stack([far ^ step for step in order] + [near])
    lg, la, pair, keep = low_products(
        core, where, ids, gates, rank, b, b_in, a, a_in, g_held, x_held, 2 * block
    )
    rest_pair, rest_keep, *first = rest_products(
        where, keep, swap(pair), lg, la, x_held, g_held, steps - 1, block, 1
    )
    rest_came = swap(rest_pair)
    send, own = first
    both, downs, ups = [], [], []
    for i, step in enumerate(order):
        if i:
            send, own = fold(where, block, i - 1, rest_keep, rest_came)
        got = flip(send, 1)
        if step == 0:
            both.append(got)
        elif step == 1:
            nearest = [flip(half, 2) for half in add_halves(own, got, (BF16, BF16))]
        elif steps != 4:
            both.append(flip(add(own, got), 2 * step))
        elif step == 3:
            passed = [flip(half, 2) for half in add_halves(own, got, (BF16, BF16))]
        else:
            mine = add_halves(own, got, (F32, F32))
            for half, came, into in zip(mine, passed, (downs, ups)):
                into.append(flip(add(half, came), 4))
    input_grad = input_gradient(lg, a, a_in)
    input_grad, both[-1] = lax.optimization_barrier((input_grad, both[-1]))
    down, up = (last(*pair) for pair in zip(total(own, both, downs, ups), nearest))
    return input_grad, down.reshape(count, rank, block), up.reshape(count, rank, block)


def plain(core, ids, gates, rank, x, g, a, b, a_in, b_in, swap):
    rows = a.shape[0]
    dot = functools.partial(lax.dot_general, preferred_element_type=F32)
    weight = gate_columns(core[0], ids, gates, 2 * rows, rank)
    both_a, both_b = jnp.concatenate([a, a_in]), jnp.concatenate([b, b_in])
    lg = (dot(both_b, g, NT) * weight).astype(BF16)
    la = (dot(both_a, x, NT) * weight).astype(BF16)
    input_grad = dot(lg, both_a, TN).astype(BF16)
    down = jnp.dot(lg, x, preferred_element_type=F32)
    up = jnp.dot(la, g, preferred_element_type=F32)
    own = jnp.concatenate([down[:rows], up[:rows]])
    other = jnp.concatenate([down[rows:], up[rows:]]).astype(BF16)
    total = lax.psum_scatter(
        own + swap(other).astype(F32), "dp", scatter_dimension=1, tiled=True
    ).reshape(2, rows // rank, rank, -1)
    return input_grad, total[0], total[1]


def solution(mesh):
    tok = P(("groups", "dp", "adapter"), None)
    return jax.shard_map(
        shards,
        mesh=mesh,
        in_specs=(tok, tok, tok, tok, P("adapter", None, None), P("adapter", None, None)),
        out_specs=(
            tok,
            P(("groups", "adapter"), None, "dp"),
            P(("groups", "adapter"), None, "dp"),
        ),
        check_vma=False,
    )
```

```python
import functools

import jax
import jax.numpy as jnp
from jax import lax
from jax.experimental import pallas as pl
from jax.experimental.pallas import tpu as pltpu
from jax.sharding import PartitionSpec as P

BF16 = jnp.bfloat16
F32 = jnp.float32
SWAP = [(0, 1), (1, 0)]
VMEM_LIMIT = 12 * 1024 * 1024
HOLD_LIMIT = 50 * 1024 * 1024
VECTORS = pl.BlockSpec(memory_space=pltpu.VMEM)
ANYWHERE = pl.BlockSpec(memory_space=pl.ANY)
SCALARS = pl.BlockSpec(memory_space=pltpu.SMEM)
NT = (((1,), (1,)), ((), ()))
TN = (((0,), (0,)), ((), ()))


def params(limit=VMEM_LIMIT):
    return pltpu.CompilerParams(vmem_limit_bytes=limit)


def cost(flops, moved):
    return pl.CostEstimate(flops=int(flops), bytes_accessed=int(moved), transcendentals=0)


def steps_of(width):
    for steps in (4, 7, 2):
        if width % (steps * 128) == 0:
            return steps
    return 1


def hold_kernel(g_hbm, x_hbm, g_ref, x_ref, sems):
    copies = [
        pltpu.make_async_copy(source.at[:, cols], target.at[:, cols], sems.at[i, j])
        for i, (source, target) in enumerate(((g_hbm, g_ref), (x_hbm, x_ref)))
        for j, cols in enumerate(tiles(g_ref.shape[1]))
    ]
    for copy in copies:
        copy.start()
    for copy in copies:
        copy.wait()


def hold(g, x):
    return pl.pallas_call(
        hold_kernel,
        in_specs=[ANYWHERE] * 2,
        out_specs=[VECTORS] * 2,
        out_shape=[jax.ShapeDtypeStruct(x.shape, BF16)] * 2,
        scratch_shapes=[pltpu.SemaphoreType.DMA((2, steps_of(x.shape[1])))],
        compiler_params=params(HOLD_LIMIT),
        cost_estimate=cost(128 * x.size, 8 * x.size),
        name="hold",
    )(g, x)


def tiles(width):
    count = steps_of(width)
    return [pl.ds(j * (width // count), width // count) for j in range(count)]


def gate_columns(core, ids, gates, rows, rank):
    total = rows // rank
    row = lax.broadcasted_iota(jnp.int32, (rows, ids.shape[1]), 0)
    adapter = (row // rank + core * (total // 2)) % total
    weight = jnp.zeros((rows, ids.shape[1]), F32)
    for k in range(ids.shape[0]):
        weight = weight + jnp.where(ids[k : k + 1, :] == adapter, gates[k : k + 1, :], 0.0)
    return weight


def store_products(where_ref, at, blocks, lows, outers, send_ref, keep_ref):
    wide = send_ref.shape[1] // blocks
    rows = send_ref.shape[0] // 2
    for j in range(blocks):
        cols = pl.ds(pl.multiple_of(where_ref[at + j] * wide, 128), wide)
        into = pl.ds(j * wide, wide)
        for i, (low, outer) in enumerate(zip(lows, outers)):
            product = jnp.dot(low, outer[:, cols], preferred_element_type=F32).astype(BF16)
            out = pl.ds(i * rows, rows)
            send_ref[out, into] = product[:rows]
            keep_ref[out, into] = product[rows:]


def factor_sum(tokens, *factors):
    total = 0.0
    for cols in tiles(tokens.shape[1]):
        rows = jnp.concatenate([factor[:, cols] for factor in factors], axis=0)
        total = total + lax.dot_general(rows, tokens[:, cols], NT, preferred_element_type=F32)
    return total


def low_kernel(rank, core_ref, where_ref, ids_ref, gates_ref, b_ref, b_in_ref, a_ref, a_in_ref, g_ref, x_ref,
               lg_ref, la_ref, send_ref, keep_ref):
    weight = gate_columns(1 - core_ref[0], ids_ref[...], gates_ref[...], 2 * b_ref.shape[0], rank)
    sums = factor_sum(g_ref, b_in_ref, b_ref), factor_sum(x_ref, a_in_ref, a_ref)
    lows = [(rows * weight).astype(BF16) for rows in sums]
    lg_ref[...], la_ref[...] = lows
    store_products(where_ref, 0, 1, lows, (x_ref, g_ref), send_ref, keep_ref)


def low_products(core, where, ids, gates, rank, b, b_in, a, a_in, g, x, wide):
    rows, width = b_in.shape
    tokens = x.shape[0]
    return pl.pallas_call(
        functools.partial(low_kernel, rank),
        in_specs=[SCALARS] * 2 + [VECTORS] * 8,
        out_specs=[VECTORS] * 4,
        out_shape=[jax.ShapeDtypeStruct((2 * rows, tokens), BF16)] * 2
        + [jax.ShapeDtypeStruct((2 * rows, wide), BF16)] * 2,
        compiler_params=params(),
        cost_estimate=cost(4 * rows * tokens * (width + 2 * wide), 4 * (rows + tokens) * width),
        name="low",
    )(core, where, ids, gates, b, b_in, a, a_in, g, x)


def rest_kernel(blocks, where_ref, lg_ref, la_ref, x_ref, g_ref, *outs):
    lows = (lg_ref[...], la_ref[...])
    for j in range(blocks):
        store_products(where_ref, 1 + j, 1, lows, (x_ref, g_ref), outs[2 * j], outs[2 * j + 1])


def rest_products(where, lg, la, x, g, blocks, wide):
    rows = lg.shape[0]
    return pl.pallas_call(
        functools.partial(rest_kernel, blocks),
        in_specs=[SCALARS] + [VECTORS] * 4,
        out_specs=[VECTORS] * (2 * blocks),
        out_shape=[jax.ShapeDtypeStruct((rows, wide), BF16)] * (2 * blocks),
        compiler_params=params(),
        cost_estimate=cost(4 * rows * x.shape[0] * blocks * wide, 8 * rows * blocks * wide),
        name="rest",
    )(where, lg, la, x, g)


def fold_kernel(block, at, where_ref, keep_ref, came_ref, send_ref, own_ref):
    near = where_ref[where_ref.shape[0] - 1]
    for place, out in ((1 - near, send_ref), (near, own_ref)):
        cols = pl.ds(pl.multiple_of((2 * at + place) * block, 128), block)
        out[...] = (keep_ref[:, cols].astype(F32) + came_ref[:, cols].astype(F32)).astype(out.dtype)


def fold(where, block, at, keep, came):
    rows = keep.shape[0]
    return pl.pallas_call(
        functools.partial(fold_kernel, block, at),
        in_specs=[SCALARS] + [VECTORS] * 2,
        out_specs=[VECTORS] * 2,
        out_shape=[
            jax.ShapeDtypeStruct((rows, block), BF16),
            jax.ShapeDtypeStruct((rows, block), F32),
        ],
        compiler_params=params(),
        cost_estimate=cost(2 * rows * block, 14 * rows * block),
        name="fold",
    )(where, keep, came)


def add_kernel(keep_ref, *refs):
    came, out_ref = refs[:-1], refs[-1]
    total = keep_ref[...]
    for ref in came:
        total = total + ref[...].astype(F32)
    out_ref[...] = total.astype(out_ref.dtype)


def add(keep, *came):
    return pl.pallas_call(
        add_kernel,
        in_specs=[VECTORS] * (1 + len(came)),
        out_specs=VECTORS,
        out_shape=jax.ShapeDtypeStruct(keep.shape, BF16),
        compiler_params=params(),
        cost_estimate=cost(keep.size, 8 * keep.size),
        name="add",
    )(keep, *came)


def halves_kernel(keep_ref, came_ref, *outs):
    rows = outs[0].shape[0]
    for half, out in enumerate(outs):
        part = pl.ds(half * rows, rows)
        out[...] = (keep_ref[part, :] + came_ref[part, :].astype(F32)).astype(out.dtype)


def add_halves(keep, came, dtypes):
    rows, block = keep.shape[0] // 2, keep.shape[1]
    return pl.pallas_call(
        halves_kernel,
        in_specs=[VECTORS] * 2,
        out_specs=[VECTORS] * 2,
        out_shape=[jax.ShapeDtypeStruct((rows, block), dtype) for dtype in dtypes],
        compiler_params=params(),
        cost_estimate=cost(keep.size, 9 * keep.size),
        name="halves",
    )(keep, came)


def total_kernel(both, downs, keep_ref, *refs):
    came, outs = refs[: len(refs) - 2], refs[len(refs) - 2 :]
    rows = outs[0].shape[0]
    for half, out in enumerate(outs):
        part = pl.ds(half * rows, rows)
        total = keep_ref[part, :]
        for ref in came[:both]:
            total = total + ref[part, :].astype(F32)
        for ref in came[both:][slice(downs) if half == 0 else slice(downs, None)]:
            total = total + ref[...].astype(F32)
        out[...] = total


def total(keep, both, downs, ups):
    rows, block = keep.shape[0] // 2, keep.shape[1]
    came = [*both, *downs, *ups]
    return pl.pallas_call(
        functools.partial(total_kernel, len(both), len(downs)),
        in_specs=[VECTORS] * (1 + len(came)),
        out_specs=[VECTORS] * 2,
        out_shape=[jax.ShapeDtypeStruct((rows, block), F32)] * 2,
        compiler_params=params(),
        cost_estimate=cost(keep.size * len(came), keep.size * (8 + 2 * len(came))),
        name="total",
    )(keep, *came)


def last_kernel(total_ref, came_ref, out_ref):
    out_ref[...] = total_ref[...] + came_ref[...].astype(F32)


def last(total, came):
    return pl.pallas_call(
        last_kernel,
        in_specs=[VECTORS] * 2,
        out_specs=VECTORS,
        out_shape=jax.ShapeDtypeStruct(total.shape, F32),
        compiler_params=params(),
        cost_estimate=cost(total.size, 10 * total.size),
        name="last",
    )(total, came)


def input_kernel(low_ref, own_ref, other_ref, out_ref):
    tile = out_ref.shape[1]
    rows = own_ref.shape[0]
    cols = pl.ds(pl.multiple_of(pl.program_id(0) * tile, 128), tile)
    dot = functools.partial(lax.dot_general, dimension_numbers=TN, preferred_element_type=F32)
    out_ref[...] = (
        dot(low_ref[:rows], other_ref[:, cols]) + dot(low_ref[rows:], own_ref[:, cols])
    ).astype(BF16)


def input_gradient(low, own, other):
    tokens = low.shape[1]
    rows, width = own.shape
    steps = steps_of(width)
    tile = width // steps
    return pl.pallas_call(
        input_kernel,
        grid=(steps,),
        in_specs=[VECTORS] * 3,
        out_specs=pl.BlockSpec((tokens, tile), lambda s: (0, s)),
        out_shape=jax.ShapeDtypeStruct((tokens, width), BF16),
        compiler_params=params(),
        cost_estimate=cost(4 * rows * tokens * width, 2 * (2 * rows + tokens) * width),
        name="input",
    )(low, own, other)


def shards(x, g, ids, gates, down_w, up_w):
    tokens, width = x.shape
    count, rank, _ = down_w.shape
    rows = count * rank
    replicas = lax.axis_size("dp")
    block = width // replicas
    core = lax.axis_index("adapter").astype(jnp.int32).reshape(1)
    a = down_w.reshape(rows, width)
    b = up_w.reshape(rows, width)
    ids, gates = ids.T, gates.T
    swap = lambda array: lax.ppermute(array, "adapter", SWAP)
    b_in = swap(b)
    me = lax.axis_index("dp").astype(jnp.int32)
    far, near = me // 2, me % 2
    flip = lambda array, by: lax.ppermute(array, "dp", [(i, i ^ by) for i in range(replicas)])
    steps = replicas // 2
    if steps < 2 or replicas & (replicas - 1) or block % 128:
        return plain(core, ids, gates, rank, x, g, a, b, swap(a), b_in, swap)

    a_in = swap(a)
    g_held, x_held = hold(g, x)
    order = list(reversed(range(steps)))
    where = jnp.stack([far ^ step for step in order] + [near])
    lg, la, pair, keep = low_products(
        core, where, ids, gates, rank, b, b_in, a, a_in, g_held, x_held, 2 * block
    )
    rest = rest_products(where, lg, la, x_held, g_held, steps - 1, 2 * block)
    terms = [(keep, swap(pair))] + [(k, swap(p)) for p, k in zip(rest[::2], rest[1::2])]
    both, downs, ups = [], [], []
    for i, step in enumerate(order):
        send, own = fold(where, block, 0, *terms[i])
        got = flip(send, 1)
        if step == 0:
            both.append(got)
        elif step == 1:
            nearest = [flip(half, 2) for half in add_halves(own, got, (BF16, BF16))]
        elif steps != 4:
            both.append(flip(add(own, got), 2 * step))
        elif step == 3:
            passed = [flip(half, 2) for half in add_halves(own, got, (BF16, BF16))]
        else:
            mine = add_halves(own, got, (F32, F32))
            for half, came, into in zip(mine, passed, (downs, ups)):
                into.append(flip(add(half, came), 4))
    input_grad = input_gradient(lg, a, a_in)
    input_grad, both[-1] = lax.optimization_barrier((input_grad, both[-1]))
    down, up = (last(*pair) for pair in zip(total(own, both, downs, ups), nearest))
    return input_grad, down.reshape(count, rank, block), up.reshape(count, rank, block)


def plain(core, ids, gates, rank, x, g, a, b, a_in, b_in, swap):
    rows = a.shape[0]
    dot = functools.partial(lax.dot_general, preferred_element_type=F32)
    weight = gate_columns(core[0], ids, gates, 2 * rows, rank)
    both_a, both_b = jnp.concatenate([a, a_in]), jnp.concatenate([b, b_in])
    lg = (dot(both_b, g, NT) * weight).astype(BF16)
    la = (dot(both_a, x, NT) * weight).astype(BF16)
    input_grad = dot(lg, both_a, TN).astype(BF16)
    down = jnp.dot(lg, x, preferred_element_type=F32)
    up = jnp.dot(la, g, preferred_element_type=F32)
    own = jnp.concatenate([down[:rows], up[:rows]])
    other = jnp.concatenate([down[rows:], up[rows:]]).astype(BF16)
    total = lax.psum_scatter(
        own + swap(other).astype(F32), "dp", scatter_dimension=1, tiled=True
    ).reshape(2, rows // rank, rank, -1)
    return input_grad, total[0], total[1]


def solution(mesh):
    tok = P(("groups", "dp", "adapter"), None)
    return jax.shard_map(
        shards,
        mesh=mesh,
        in_specs=(tok, tok, tok, tok, P("adapter", None, None), P("adapter", None, None)),
        out_specs=(
            tok,
            P(("groups", "adapter"), None, "dp"),
            P(("groups", "adapter"), None, "dp"),
        ),
        check_vma=False,
    )
```

```python
import functools

import jax
import jax.numpy as jnp
from jax import lax
from jax.experimental import pallas as pl
from jax.experimental.pallas import tpu as pltpu
from jax.sharding import PartitionSpec as P

BF16 = jnp.bfloat16
F32 = jnp.float32
SWAP = [(0, 1), (1, 0)]
VMEM_LIMIT = 12 * 1024 * 1024
HOLD_LIMIT = 50 * 1024 * 1024
VECTORS = pl.BlockSpec(memory_space=pltpu.VMEM)
ANYWHERE = pl.BlockSpec(memory_space=pl.ANY)
NT = (((1,), (1,)), ((), ()))
TN = (((0,), (0,)), ((), ()))


def params(limit=VMEM_LIMIT):
    return pltpu.CompilerParams(vmem_limit_bytes=limit)


def cost(flops, moved):
    return pl.CostEstimate(flops=int(flops), bytes_accessed=int(moved), transcendentals=0)


def steps_of(width):
    for steps in (4, 7, 2):
        if width % (steps * 128) == 0:
            return steps
    return 1


def hold_kernel(g_hbm, x_hbm, g_ref, x_ref, sems):
    copies = [
        pltpu.make_async_copy(source.at[:, cols], target.at[:, cols], sems.at[i, j])
        for i, (source, target) in enumerate(((g_hbm, g_ref), (x_hbm, x_ref)))
        for j, cols in enumerate(tiles(g_ref.shape[1]))
    ]
    for copy in copies:
        copy.start()
    for copy in copies:
        copy.wait()


def hold(g, x):
    return pl.pallas_call(
        hold_kernel,
        in_specs=[ANYWHERE] * 2,
        out_specs=[VECTORS] * 2,
        out_shape=[jax.ShapeDtypeStruct(x.shape, BF16)] * 2,
        scratch_shapes=[pltpu.SemaphoreType.DMA((2, steps_of(x.shape[1])))],
        compiler_params=params(HOLD_LIMIT),
        cost_estimate=cost(128 * x.size, 8 * x.size),
        name="hold",
    )(g, x)


def tiles(width):
    count = steps_of(width)
    return [pl.ds(j * (width // count), width // count) for j in range(count)]


def gate_columns(core, ids, gates, rows, rank):
    total = rows // rank
    row = lax.broadcasted_iota(jnp.int32, (rows, ids.shape[1]), 0)
    adapter = (row // rank + core * (total // 2)) % total
    weight = jnp.zeros((rows, ids.shape[1]), F32)
    for k in range(ids.shape[0]):
        weight = weight + jnp.where(ids[k : k + 1, :] == adapter, gates[k : k + 1, :], 0.0)
    return weight


class Places:
    def __init__(self, pairs):
        self.pairs = pairs

    def far(self, j):
        return (lax.axis_index("dp") >> 1) ^ (self.pairs - 1 - j)

    def near(self):
        return lax.axis_index("dp") & 1


def store_products(places, at, blocks, lows, outers, send_ref, keep_ref):
    wide = send_ref.shape[1] // blocks
    rows = send_ref.shape[0] // 2
    for j in range(blocks):
        cols = pl.ds(pl.multiple_of(places.far(at + j) * wide, 128), wide)
        into = pl.ds(j * wide, wide)
        for i, (low, outer) in enumerate(zip(lows, outers)):
            product = jnp.dot(low, outer[:, cols], preferred_element_type=F32).astype(BF16)
            out = pl.ds(i * rows, rows)
            send_ref[out, into] = product[:rows]
            keep_ref[out, into] = product[rows:]


def factor_sum(tokens, *factors):
    total = 0.0
    for cols in tiles(tokens.shape[1]):
        rows = jnp.concatenate([factor[:, cols] for factor in factors], axis=0)
        total = total + lax.dot_general(rows, tokens[:, cols], NT, preferred_element_type=F32)
    return total


def low_kernel(rank, places, ids_ref, gates_ref, b_ref, b_in_ref, a_ref, a_in_ref, g_ref, x_ref,
               lg_ref, la_ref, send_ref, keep_ref):
    weight = gate_columns(1 - lax.axis_index("adapter"), ids_ref[...], gates_ref[...], 2 * b_ref.shape[0], rank)
    sums = factor_sum(g_ref, b_in_ref, b_ref), factor_sum(x_ref, a_in_ref, a_ref)
    lows = [(rows * weight).astype(BF16) for rows in sums]
    lg_ref[...], la_ref[...] = lows
    store_products(places, 0, 1, lows, (x_ref, g_ref), send_ref, keep_ref)


def low_products(places, ids, gates, rank, b, b_in, a, a_in, g, x, wide):
    rows, width = b_in.shape
    tokens = x.shape[0]
    return pl.pallas_call(
        functools.partial(low_kernel, rank, places),
        in_specs=[VECTORS] * 8,
        out_specs=[VECTORS] * 4,
        out_shape=[jax.ShapeDtypeStruct((2 * rows, tokens), BF16)] * 2
        + [jax.ShapeDtypeStruct((2 * rows, wide), BF16)] * 2,
        compiler_params=params(),
        cost_estimate=cost(4 * rows * tokens * (width + 2 * wide), 4 * (rows + tokens) * width),
        name="low",
    )(ids, gates, b, b_in, a, a_in, g, x)


def rest_kernel(blocks, places, lg_ref, la_ref, x_ref, g_ref, *outs):
    lows = (lg_ref[...], la_ref[...])
    for j in range(blocks):
        store_products(places, 1 + j, 1, lows, (x_ref, g_ref), outs[2 * j], outs[2 * j + 1])


def rest_products(places, lg, la, x, g, blocks, wide):
    rows = lg.shape[0]
    return pl.pallas_call(
        functools.partial(rest_kernel, blocks, places),
        in_specs=[VECTORS] * 4,
        out_specs=[VECTORS] * (2 * blocks),
        out_shape=[jax.ShapeDtypeStruct((rows, wide), BF16)] * (2 * blocks),
        compiler_params=params(),
        cost_estimate=cost(4 * rows * x.shape[0] * blocks * wide, 8 * rows * blocks * wide),
        name="rest",
    )(lg, la, x, g)


def fold_kernel(block, at, places, keep_ref, came_ref, send_ref, own_ref):
    near = places.near()
    for place, out in ((1 - near, send_ref), (near, own_ref)):
        cols = pl.ds(pl.multiple_of((2 * at + place) * block, 128), block)
        out[...] = (keep_ref[:, cols].astype(F32) + came_ref[:, cols].astype(F32)).astype(out.dtype)


def fold(places, block, at, keep, came):
    rows = keep.shape[0]
    return pl.pallas_call(
        functools.partial(fold_kernel, block, at, places),
        in_specs=[VECTORS] * 2,
        out_specs=[VECTORS] * 2,
        out_shape=[
            jax.ShapeDtypeStruct((rows, block), BF16),
            jax.ShapeDtypeStruct((rows, block), F32),
        ],
        compiler_params=params(),
        cost_estimate=cost(2 * rows * block, 14 * rows * block),
        name="fold",
    )(keep, came)


def add_kernel(keep_ref, *refs):
    came, out_ref = refs[:-1], refs[-1]
    total = keep_ref[...]
    for ref in came:
        total = total + ref[...].astype(F32)
    out_ref[...] = total.astype(out_ref.dtype)


def add(keep, *came):
    return pl.pallas_call(
        add_kernel,
        in_specs=[VECTORS] * (1 + len(came)),
        out_specs=VECTORS,
        out_shape=jax.ShapeDtypeStruct(keep.shape, BF16),
        compiler_params=params(),
        cost_estimate=cost(keep.size, 8 * keep.size),
        name="add",
    )(keep, *came)


def halves_kernel(keep_ref, came_ref, *outs):
    rows = outs[0].shape[0]
    for half, out in enumerate(outs):
        part = pl.ds(half * rows, rows)
        out[...] = (keep_ref[part, :] + came_ref[part, :].astype(F32)).astype(out.dtype)


def add_halves(keep, came, dtypes):
    rows, block = keep.shape[0] // 2, keep.shape[1]
    return pl.pallas_call(
        halves_kernel,
        in_specs=[VECTORS] * 2,
        out_specs=[VECTORS] * 2,
        out_shape=[jax.ShapeDtypeStruct((rows, block), dtype) for dtype in dtypes],
        compiler_params=params(),
        cost_estimate=cost(keep.size, 9 * keep.size),
        name="halves",
    )(keep, came)


def total_kernel(both, downs, keep_ref, *refs):
    came, outs = refs[: len(refs) - 2], refs[len(refs) - 2 :]
    rows = outs[0].shape[0]
    for half, out in enumerate(outs):
        part = pl.ds(half * rows, rows)
        total = keep_ref[part, :]
        for ref in came[:both]:
            total = total + ref[part, :].astype(F32)
        for ref in came[both:][slice(downs) if half == 0 else slice(downs, None)]:
            total = total + ref[...].astype(F32)
        out[...] = total


def total(keep, both, downs, ups):
    rows, block = keep.shape[0] // 2, keep.shape[1]
    came = [*both, *downs, *ups]
    return pl.pallas_call(
        functools.partial(total_kernel, len(both), len(downs)),
        in_specs=[VECTORS] * (1 + len(came)),
        out_specs=[VECTORS] * 2,
        out_shape=[jax.ShapeDtypeStruct((rows, block), F32)] * 2,
        compiler_params=params(),
        cost_estimate=cost(keep.size * len(came), keep.size * (8 + 2 * len(came))),
        name="total",
    )(keep, *came)


def last_kernel(total_ref, came_ref, out_ref):
    out_ref[...] = total_ref[...] + came_ref[...].astype(F32)


def last(total, came):
    return pl.pallas_call(
        last_kernel,
        in_specs=[VECTORS] * 2,
        out_specs=VECTORS,
        out_shape=jax.ShapeDtypeStruct(total.shape, F32),
        compiler_params=params(),
        cost_estimate=cost(total.size, 10 * total.size),
        name="last",
    )(total, came)


def input_kernel(low_ref, own_ref, other_ref, out_ref):
    tile = out_ref.shape[1]
    rows = own_ref.shape[0]
    cols = pl.ds(pl.multiple_of(pl.program_id(0) * tile, 128), tile)
    dot = functools.partial(lax.dot_general, dimension_numbers=TN, preferred_element_type=F32)
    out_ref[...] = (
        dot(low_ref[:rows], other_ref[:, cols]) + dot(low_ref[rows:], own_ref[:, cols])
    ).astype(BF16)


def input_gradient(low, own, other):
    tokens = low.shape[1]
    rows, width = own.shape
    steps = steps_of(width)
    tile = width // steps
    return pl.pallas_call(
        input_kernel,
        grid=(steps,),
        in_specs=[VECTORS] * 3,
        out_specs=pl.BlockSpec((tokens, tile), lambda s: (0, s)),
        out_shape=jax.ShapeDtypeStruct((tokens, width), BF16),
        compiler_params=params(),
        cost_estimate=cost(4 * rows * tokens * width, 2 * (2 * rows + tokens) * width),
        name="input",
    )(low, own, other)


def shards(x, g, ids, gates, down_w, up_w):
    tokens, width = x.shape
    count, rank, _ = down_w.shape
    rows = count * rank
    replicas = lax.axis_size("dp")
    block = width // replicas
    core = lax.axis_index("adapter")
    a = down_w.reshape(rows, width)
    b = up_w.reshape(rows, width)
    ids, gates = ids.T, gates.T
    swap = lambda array: lax.ppermute(array, "adapter", SWAP)
    b_in = swap(b)
    flip = lambda array, by: lax.ppermute(array, "dp", [(i, i ^ by) for i in range(replicas)])
    steps = replicas // 2
    if steps < 2 or replicas & (replicas - 1) or block % 128:
        return plain(core, ids, gates, rank, x, g, a, b, swap(a), b_in, swap)

    a_in = swap(a)
    g_held, x_held = hold(g, x)
    order = list(reversed(range(steps)))
    places = Places(steps)
    lg, la, pair, keep = low_products(
        places, ids, gates, rank, b, b_in, a, a_in, g_held, x_held, 2 * block
    )
    rest = rest_products(places, lg, la, x_held, g_held, steps - 1, 2 * block)
    terms = [(keep, swap(pair))] + [(k, swap(p)) for p, k in zip(rest[::2], rest[1::2])]
    both, downs, ups = [], [], []
    for i, step in enumerate(order):
        send, own = fold(places, block, 0, *terms[i])
        got = flip(send, 1)
        if step == 0:
            both.append(got)
        elif step == 1:
            nearest = [flip(half, 2) for half in add_halves(own, got, (BF16, BF16))]
        elif steps != 4:
            both.append(flip(add(own, got), 2 * step))
        elif step == 3:
            passed = [flip(half, 2) for half in add_halves(own, got, (BF16, BF16))]
        else:
            mine = add_halves(own, got, (F32, F32))
            for half, came, into in zip(mine, passed, (downs, ups)):
                into.append(flip(add(half, came), 4))
    input_grad = input_gradient(lg, a, a_in)
    input_grad, both[-1] = lax.optimization_barrier((input_grad, both[-1]))
    down, up = (last(*pair) for pair in zip(total(own, both, downs, ups), nearest))
    return input_grad, down.reshape(count, rank, block), up.reshape(count, rank, block)


def plain(core, ids, gates, rank, x, g, a, b, a_in, b_in, swap):
    rows = a.shape[0]
    dot = functools.partial(lax.dot_general, preferred_element_type=F32)
    weight = gate_columns(core, ids, gates, 2 * rows, rank)
    both_a, both_b = jnp.concatenate([a, a_in]), jnp.concatenate([b, b_in])
    lg = (dot(both_b, g, NT) * weight).astype(BF16)
    la = (dot(both_a, x, NT) * weight).astype(BF16)
    input_grad = dot(lg, both_a, TN).astype(BF16)
    down = jnp.dot(lg, x, preferred_element_type=F32)
    up = jnp.dot(la, g, preferred_element_type=F32)
    own = jnp.concatenate([down[:rows], up[:rows]])
    other = jnp.concatenate([down[rows:], up[rows:]]).astype(BF16)
    total = lax.psum_scatter(
        own + swap(other).astype(F32), "dp", scatter_dimension=1, tiled=True
    ).reshape(2, rows // rank, rank, -1)
    return input_grad, total[0], total[1]


def solution(mesh):
    tok = P(("groups", "dp", "adapter"), None)
    return jax.shard_map(
        shards,
        mesh=mesh,
        in_specs=(tok, tok, tok, tok, P("adapter", None, None), P("adapter", None, None)),
        out_specs=(
            tok,
            P(("groups", "adapter"), None, "dp"),
            P(("groups", "adapter"), None, "dp"),
        ),
        check_vma=False,
    )
```

```python
import functools

import jax
import jax.numpy as jnp
from jax import lax
from jax.experimental import pallas as pl
from jax.experimental.pallas import tpu as pltpu
from jax.sharding import PartitionSpec as P

BF16 = jnp.bfloat16
F32 = jnp.float32
SWAP = [(0, 1), (1, 0)]
VMEM_LIMIT = 12 * 1024 * 1024
HOLD_LIMIT = 50 * 1024 * 1024
VECTORS = pl.BlockSpec(memory_space=pltpu.VMEM)
ANYWHERE = pl.BlockSpec(memory_space=pl.ANY)
NT = (((1,), (1,)), ((), ()))
TN = (((0,), (0,)), ((), ()))


def params(limit=VMEM_LIMIT):
    return pltpu.CompilerParams(vmem_limit_bytes=limit)


def cost(flops, moved):
    return pl.CostEstimate(flops=int(flops), bytes_accessed=int(moved), transcendentals=0)


def steps_of(width):
    for steps in (4, 7, 2):
        if width % (steps * 128) == 0:
            return steps
    return 1


def hold_kernel(g_hbm, x_hbm, g_ref, x_ref, sems):
    copies = [
        pltpu.make_async_copy(source.at[:, cols], target.at[:, cols], sems.at[i, j])
        for i, (source, target) in enumerate(((g_hbm, g_ref), (x_hbm, x_ref)))
        for j, cols in enumerate(tiles(g_ref.shape[1]))
    ]
    for copy in copies:
        copy.start()
    for copy in copies:
        copy.wait()


def hold(g, x):
    return pl.pallas_call(
        hold_kernel,
        in_specs=[ANYWHERE] * 2,
        out_specs=[VECTORS] * 2,
        out_shape=[jax.ShapeDtypeStruct(x.shape, BF16)] * 2,
        scratch_shapes=[pltpu.SemaphoreType.DMA((2, steps_of(x.shape[1])))],
        compiler_params=params(HOLD_LIMIT),
        cost_estimate=cost(128 * x.size, 8 * x.size),
        name="hold",
    )(g, x)


def tiles(width):
    count = steps_of(width)
    return [pl.ds(j * (width // count), width // count) for j in range(count)]


def gate_columns(core, ids, gates, rows, rank):
    total = rows // rank
    row = lax.broadcasted_iota(jnp.int32, (rows, ids.shape[1]), 0)
    adapter = (row // rank + core * (total // 2)) % total
    weight = jnp.zeros((rows, ids.shape[1]), F32)
    for k in range(ids.shape[0]):
        weight = weight + jnp.where(ids[k : k + 1, :] == adapter, gates[k : k + 1, :], 0.0)
    return weight


class Places:
    def __init__(self, pairs):
        self.pairs = pairs

    def far(self, j):
        return (lax.axis_index("dp") >> 1) ^ (self.pairs - 1 - j)

    def near(self):
        return lax.axis_index("dp") & 1


def store_products(places, at, blocks, lows, outers, send_ref, keep_ref):
    wide = send_ref.shape[1] // blocks
    rows = send_ref.shape[0] // 2
    for j in range(blocks):
        cols = pl.ds(pl.multiple_of(places.far(at + j) * wide, 128), wide)
        into = pl.ds(j * wide, wide)
        for i, (low, outer) in enumerate(zip(lows, outers)):
            product = jnp.dot(low, outer[:, cols], preferred_element_type=F32).astype(BF16)
            out = pl.ds(i * rows, rows)
            send_ref[out, into] = product[:rows]
            keep_ref[out, into] = product[rows:]


def factor_sum(tokens, *factors):
    total = 0.0
    for cols in tiles(tokens.shape[1]):
        rows = jnp.concatenate([factor[:, cols] for factor in factors], axis=0)
        total = total + lax.dot_general(rows, tokens[:, cols], NT, preferred_element_type=F32)
    return total


def low_kernel(rank, ids_ref, gates_ref, own_ref, other_ref, tokens_ref, low_ref):
    core = 1 - lax.axis_index("adapter")
    weight = gate_columns(core, ids_ref[...], gates_ref[...], low_ref.shape[0], rank)
    low_ref[...] = (factor_sum(tokens_ref, other_ref, own_ref) * weight).astype(BF16)


def low_product(ids, gates, rank, own, other, tokens):
    rows, width = own.shape
    count = tokens.shape[0]
    return pl.pallas_call(
        functools.partial(low_kernel, rank),
        in_specs=[VECTORS] * 5,
        out_specs=VECTORS,
        out_shape=jax.ShapeDtypeStruct((2 * rows, count), BF16),
        compiler_params=params(),
        cost_estimate=cost(4 * rows * count * width, 2 * (2 * rows + count) * width),
        name="low",
    )(ids, gates, own, other, tokens)


def first_kernel(rank, places, ids_ref, gates_ref, own_ref, other_ref, la_ref, g_ref, x_ref,
                 lg_ref, send_ref, keep_ref):
    low_kernel(rank, ids_ref, gates_ref, own_ref, other_ref, g_ref, lg_ref)
    lows = (lg_ref[...], la_ref[...])
    store_products(places, 0, 1, lows, (x_ref, g_ref), send_ref, keep_ref)


def first_products(places, ids, gates, rank, own, other, la, g, x, wide):
    rows, width = own.shape
    count = x.shape[0]
    return pl.pallas_call(
        functools.partial(first_kernel, rank, places),
        in_specs=[VECTORS] * 7,
        out_specs=[VECTORS] * 3,
        out_shape=[jax.ShapeDtypeStruct((2 * rows, count), BF16)]
        + [jax.ShapeDtypeStruct((2 * rows, wide), BF16)] * 2,
        compiler_params=params(),
        cost_estimate=cost(4 * rows * count * (width + 2 * wide), 2 * (2 * rows + count) * width),
        name="first",
    )(ids, gates, own, other, la, g, x)


def rest_kernel(blocks, places, lg_ref, la_ref, x_ref, g_ref, *outs):
    lows = (lg_ref[...], la_ref[...])
    for j in range(blocks):
        store_products(places, 1 + j, 1, lows, (x_ref, g_ref), outs[2 * j], outs[2 * j + 1])


def rest_products(places, lg, la, x, g, blocks, wide):
    rows = lg.shape[0]
    return pl.pallas_call(
        functools.partial(rest_kernel, blocks, places),
        in_specs=[VECTORS] * 4,
        out_specs=[VECTORS] * (2 * blocks),
        out_shape=[jax.ShapeDtypeStruct((rows, wide), BF16)] * (2 * blocks),
        compiler_params=params(),
        cost_estimate=cost(4 * rows * x.shape[0] * blocks * wide, 8 * rows * blocks * wide),
        name="rest",
    )(lg, la, x, g)


def fold_kernel(block, at, places, keep_ref, came_ref, send_ref, own_ref):
    near = places.near()
    for place, out in ((1 - near, send_ref), (near, own_ref)):
        cols = pl.ds(pl.multiple_of((2 * at + place) * block, 128), block)
        out[...] = (keep_ref[:, cols].astype(F32) + came_ref[:, cols].astype(F32)).astype(out.dtype)


def fold(places, block, at, keep, came):
    rows = keep.shape[0]
    return pl.pallas_call(
        functools.partial(fold_kernel, block, at, places),
        in_specs=[VECTORS] * 2,
        out_specs=[VECTORS] * 2,
        out_shape=[
            jax.ShapeDtypeStruct((rows, block), BF16),
            jax.ShapeDtypeStruct((rows, block), F32),
        ],
        compiler_params=params(),
        cost_estimate=cost(2 * rows * block, 14 * rows * block),
        name="fold",
    )(keep, came)


def add_kernel(keep_ref, *refs):
    came, out_ref = refs[:-1], refs[-1]
    total = keep_ref[...]
    for ref in came:
        total = total + ref[...].astype(F32)
    out_ref[...] = total.astype(out_ref.dtype)


def add(keep, *came):
    return pl.pallas_call(
        add_kernel,
        in_specs=[VECTORS] * (1 + len(came)),
        out_specs=VECTORS,
        out_shape=jax.ShapeDtypeStruct(keep.shape, BF16),
        compiler_params=params(),
        cost_estimate=cost(keep.size, 8 * keep.size),
        name="add",
    )(keep, *came)


def halves_kernel(keep_ref, came_ref, *outs):
    rows = outs[0].shape[0]
    for half, out in enumerate(outs):
        part = pl.ds(half * rows, rows)
        out[...] = (keep_ref[part, :] + came_ref[part, :].astype(F32)).astype(out.dtype)


def add_halves(keep, came, dtypes):
    rows, block = keep.shape[0] // 2, keep.shape[1]
    return pl.pallas_call(
        halves_kernel,
        in_specs=[VECTORS] * 2,
        out_specs=[VECTORS] * 2,
        out_shape=[jax.ShapeDtypeStruct((rows, block), dtype) for dtype in dtypes],
        compiler_params=params(),
        cost_estimate=cost(keep.size, 9 * keep.size),
        name="halves",
    )(keep, came)


def total_kernel(both, downs, keep_ref, *refs):
    came, outs = refs[: len(refs) - 2], refs[len(refs) - 2 :]
    rows = outs[0].shape[0]
    for half, out in enumerate(outs):
        part = pl.ds(half * rows, rows)
        total = keep_ref[part, :]
        for ref in came[:both]:
            total = total + ref[part, :].astype(F32)
        for ref in came[both:][slice(downs) if half == 0 else slice(downs, None)]:
            total = total + ref[...].astype(F32)
        out[...] = total


def total(keep, both, downs, ups):
    rows, block = keep.shape[0] // 2, keep.shape[1]
    came = [*both, *downs, *ups]
    return pl.pallas_call(
        functools.partial(total_kernel, len(both), len(downs)),
        in_specs=[VECTORS] * (1 + len(came)),
        out_specs=[VECTORS] * 2,
        out_shape=[jax.ShapeDtypeStruct((rows, block), F32)] * 2,
        compiler_params=params(),
        cost_estimate=cost(keep.size * len(came), keep.size * (8 + 2 * len(came))),
        name="total",
    )(keep, *came)


def last_kernel(total_ref, came_ref, out_ref):
    out_ref[...] = total_ref[...] + came_ref[...].astype(F32)


def last(total, came):
    return pl.pallas_call(
        last_kernel,
        in_specs=[VECTORS] * 2,
        out_specs=VECTORS,
        out_shape=jax.ShapeDtypeStruct(total.shape, F32),
        compiler_params=params(),
        cost_estimate=cost(total.size, 10 * total.size),
        name="last",
    )(total, came)


def input_kernel(low_ref, own_ref, other_ref, out_ref):
    tile = out_ref.shape[1]
    rows = own_ref.shape[0]
    cols = pl.ds(pl.multiple_of(pl.program_id(0) * tile, 128), tile)
    dot = functools.partial(lax.dot_general, dimension_numbers=TN, preferred_element_type=F32)
    out_ref[...] = (
        dot(low_ref[:rows], other_ref[:, cols]) + dot(low_ref[rows:], own_ref[:, cols])
    ).astype(BF16)


def input_gradient(low, own, other):
    tokens = low.shape[1]
    rows, width = own.shape
    steps = steps_of(width)
    tile = width // steps
    return pl.pallas_call(
        input_kernel,
        grid=(steps,),
        in_specs=[VECTORS] * 3,
        out_specs=pl.BlockSpec((tokens, tile), lambda s: (0, s)),
        out_shape=jax.ShapeDtypeStruct((tokens, width), BF16),
        compiler_params=params(),
        cost_estimate=cost(4 * rows * tokens * width, 2 * (2 * rows + tokens) * width),
        name="input",
    )(low, own, other)


def shards(x, g, ids, gates, down_w, up_w):
    tokens, width = x.shape
    count, rank, _ = down_w.shape
    rows = count * rank
    replicas = lax.axis_size("dp")
    block = width // replicas
    core = lax.axis_index("adapter")
    a = down_w.reshape(rows, width)
    b = up_w.reshape(rows, width)
    ids, gates = ids.T, gates.T
    swap = lambda array: lax.ppermute(array, "adapter", SWAP)
    b_in = swap(b)
    flip = lambda array, by: lax.ppermute(array, "dp", [(i, i ^ by) for i in range(replicas)])
    steps = replicas // 2
    if steps < 2 or replicas & (replicas - 1) or block % 128:
        return plain(core, ids, gates, rank, x, g, a, b, swap(a), b_in, swap)

    a_in = swap(a)
    g_held, x_held = hold(g, x)
    order = list(reversed(range(steps)))
    places = Places(steps)
    la = low_product(ids, gates, rank, a, a_in, x_held)
    lg, pair, keep = first_products(
        places, ids, gates, rank, b, b_in, la, g_held, x_held, 2 * block
    )
    rest = rest_products(places, lg, la, x_held, g_held, steps - 1, 2 * block)
    terms = [(keep, swap(pair))] + [(k, swap(p)) for p, k in zip(rest[::2], rest[1::2])]
    both, downs, ups = [], [], []
    for i, step in enumerate(order):
        send, own = fold(places, block, 0, *terms[i])
        got = flip(send, 1)
        if step == 0:
            both.append(got)
        elif step == 1:
            nearest = [flip(half, 2) for half in add_halves(own, got, (BF16, BF16))]
        elif steps != 4:
            both.append(flip(add(own, got), 2 * step))
        elif step == 3:
            passed = [flip(half, 2) for half in add_halves(own, got, (BF16, BF16))]
        else:
            mine = add_halves(own, got, (F32, F32))
            for half, came, into in zip(mine, passed, (downs, ups)):
                into.append(flip(add(half, came), 4))
    input_grad = input_gradient(lg, a, a_in)
    input_grad, both[-1] = lax.optimization_barrier((input_grad, both[-1]))
    down, up = (last(*pair) for pair in zip(total(own, both, downs, ups), nearest))
    return input_grad, down.reshape(count, rank, block), up.reshape(count, rank, block)


def plain(core, ids, gates, rank, x, g, a, b, a_in, b_in, swap):
    rows = a.shape[0]
    dot = functools.partial(lax.dot_general, preferred_element_type=F32)
    weight = gate_columns(core, ids, gates, 2 * rows, rank)
    both_a, both_b = jnp.concatenate([a, a_in]), jnp.concatenate([b, b_in])
    lg = (dot(both_b, g, NT) * weight).astype(BF16)
    la = (dot(both_a, x, NT) * weight).astype(BF16)
    input_grad = dot(lg, both_a, TN).astype(BF16)
    down = jnp.dot(lg, x, preferred_element_type=F32)
    up = jnp.dot(la, g, preferred_element_type=F32)
    own = jnp.concatenate([down[:rows], up[:rows]])
    other = jnp.concatenate([down[rows:], up[rows:]]).astype(BF16)
    total = lax.psum_scatter(
        own + swap(other).astype(F32), "dp", scatter_dimension=1, tiled=True
    ).reshape(2, rows // rank, rank, -1)
    return input_grad, total[0], total[1]


def solution(mesh):
    tok = P(("groups", "dp", "adapter"), None)
    return jax.shard_map(
        shards,
        mesh=mesh,
        in_specs=(tok, tok, tok, tok, P("adapter", None, None), P("adapter", None, None)),
        out_specs=(
            tok,
            P(("groups", "adapter"), None, "dp"),
            P(("groups", "adapter"), None, "dp"),
        ),
        check_vma=False,
    )
```

```python
import functools

import jax
import jax.numpy as jnp
from jax import lax
from jax.experimental import pallas as pl
from jax.experimental.pallas import tpu as pltpu
from jax.sharding import PartitionSpec as P

BF16 = jnp.bfloat16
F32 = jnp.float32
SWAP = [(0, 1), (1, 0)]
VMEM_LIMIT = 12 * 1024 * 1024
HOLD_LIMIT = 50 * 1024 * 1024
VECTORS = pl.BlockSpec(memory_space=pltpu.VMEM)
ANYWHERE = pl.BlockSpec(memory_space=pl.ANY)
NT = (((1,), (1,)), ((), ()))
TN = (((0,), (0,)), ((), ()))


def params(limit=VMEM_LIMIT):
    return pltpu.CompilerParams(vmem_limit_bytes=limit)


def cost(flops, moved):
    return pl.CostEstimate(flops=int(flops), bytes_accessed=int(moved), transcendentals=0)


def steps_of(width):
    for steps in (4, 7, 2):
        if width % (steps * 128) == 0:
            return steps
    return 1


def hold_kernel(g_hbm, x_hbm, g_ref, x_ref, sems):
    copies = [
        pltpu.make_async_copy(source.at[:, cols], target.at[:, cols], sems.at[i, j])
        for i, (source, target) in enumerate(((g_hbm, g_ref), (x_hbm, x_ref)))
        for j, cols in enumerate(tiles(g_ref.shape[1]))
    ]
    for copy in copies:
        copy.start()
    for copy in copies:
        copy.wait()


def hold(g, x):
    return pl.pallas_call(
        hold_kernel,
        in_specs=[ANYWHERE] * 2,
        out_specs=[VECTORS] * 2,
        out_shape=[jax.ShapeDtypeStruct(x.shape, BF16)] * 2,
        scratch_shapes=[pltpu.SemaphoreType.DMA((2, steps_of(x.shape[1])))],
        compiler_params=params(HOLD_LIMIT),
        cost_estimate=cost(128 * x.size, 8 * x.size),
        name="hold",
    )(g, x)


def tiles(width):
    count = steps_of(width)
    return [pl.ds(j * (width // count), width // count) for j in range(count)]


def gate_columns(core, ids, gates, rows, rank):
    total = rows // rank
    row = lax.broadcasted_iota(jnp.int32, (rows, ids.shape[1]), 0)
    adapter = (row // rank + core * (total // 2)) % total
    weight = jnp.zeros((rows, ids.shape[1]), F32)
    for k in range(ids.shape[0]):
        weight = weight + jnp.where(ids[k : k + 1, :] == adapter, gates[k : k + 1, :], 0.0)
    return weight


class Places:
    def __init__(self, pairs):
        self.pairs = pairs

    def far(self, j):
        return (lax.axis_index("dp") >> 1) ^ (self.pairs - 1 - j)

    def near(self):
        return lax.axis_index("dp") & 1


def store_products(places, at, blocks, lows, outers, send_ref, keep_ref):
    wide = send_ref.shape[1] // blocks
    rows = send_ref.shape[0] // 2
    for j in range(blocks):
        cols = pl.ds(pl.multiple_of(places.far(at + j) * wide, 128), wide)
        into = pl.ds(j * wide, wide)
        for i, (low, outer) in enumerate(zip(lows, outers)):
            product = jnp.dot(low, outer[:, cols], preferred_element_type=F32).astype(BF16)
            out = pl.ds(i * rows, rows)
            send_ref[out, into] = product[:rows]
            keep_ref[out, into] = product[rows:]


def factor_sum(tokens, *factors):
    total = 0.0
    for cols in tiles(tokens.shape[1]):
        rows = jnp.concatenate([factor[:, cols] for factor in factors], axis=0)
        total = total + lax.dot_general(rows, tokens[:, cols], NT, preferred_element_type=F32)
    return total


def low_kernel(rank, places, ids_ref, gates_ref, b_ref, b_in_ref, a_ref, a_in_ref, g_ref, x_ref,
               lg_ref, la_ref, send_ref, keep_ref):
    weight = gate_columns(1 - lax.axis_index("adapter"), ids_ref[...], gates_ref[...], 2 * b_ref.shape[0], rank)
    sums = factor_sum(g_ref, b_in_ref, b_ref), factor_sum(x_ref, a_in_ref, a_ref)
    lows = [(rows * weight).astype(BF16) for rows in sums]
    lg_ref[...], la_ref[...] = lows
    store_products(places, 0, 1, lows, (x_ref, g_ref), send_ref, keep_ref)


def low_products(places, ids, gates, rank, b, b_in, a, a_in, g, x, wide):
    rows, width = b_in.shape
    tokens = x.shape[0]
    return pl.pallas_call(
        functools.partial(low_kernel, rank, places),
        in_specs=[VECTORS] * 8,
        out_specs=[VECTORS] * 4,
        out_shape=[jax.ShapeDtypeStruct((2 * rows, tokens), BF16)] * 2
        + [jax.ShapeDtypeStruct((2 * rows, wide), BF16)] * 2,
        compiler_params=params(),
        cost_estimate=cost(4 * rows * tokens * (width + 2 * wide), 4 * (rows + tokens) * width),
        name="low",
    )(ids, gates, b, b_in, a, a_in, g, x)


def rest_kernel(blocks, places, lg_ref, la_ref, x_ref, g_ref, *outs):
    lows = (lg_ref[...], la_ref[...])
    for j in range(blocks):
        store_products(places, 1 + j, 1, lows, (x_ref, g_ref), outs[2 * j], outs[2 * j + 1])


def rest_products(places, lg, la, x, g, blocks, wide):
    rows = lg.shape[0]
    return pl.pallas_call(
        functools.partial(rest_kernel, blocks, places),
        in_specs=[VECTORS] * 4,
        out_specs=[VECTORS] * (2 * blocks),
        out_shape=[jax.ShapeDtypeStruct((rows, wide), BF16)] * (2 * blocks),
        compiler_params=params(),
        cost_estimate=cost(4 * rows * x.shape[0] * blocks * wide, 8 * rows * blocks * wide),
        name="rest",
    )(lg, la, x, g)


def fold_kernel(block, at, places, keep_ref, came_ref, send_ref, own_ref):
    near = places.near()
    for place, out in ((1 - near, send_ref), (near, own_ref)):
        cols = pl.ds(pl.multiple_of((2 * at + place) * block, 128), block)
        out[...] = (keep_ref[:, cols].astype(F32) + came_ref[:, cols].astype(F32)).astype(out.dtype)


def fold(places, block, at, keep, came):
    rows = keep.shape[0]
    return pl.pallas_call(
        functools.partial(fold_kernel, block, at, places),
        in_specs=[VECTORS] * 2,
        out_specs=[VECTORS] * 2,
        out_shape=[
            jax.ShapeDtypeStruct((rows, block), BF16),
            jax.ShapeDtypeStruct((rows, block), F32),
        ],
        compiler_params=params(),
        cost_estimate=cost(2 * rows * block, 14 * rows * block),
        name="fold",
    )(keep, came)


def add_kernel(keep_ref, *refs):
    came, out_ref = refs[:-1], refs[-1]
    total = keep_ref[...]
    for ref in came:
        total = total + ref[...].astype(F32)
    out_ref[...] = total.astype(out_ref.dtype)


def add(keep, *came):
    return pl.pallas_call(
        add_kernel,
        in_specs=[VECTORS] * (1 + len(came)),
        out_specs=VECTORS,
        out_shape=jax.ShapeDtypeStruct(keep.shape, BF16),
        compiler_params=params(),
        cost_estimate=cost(keep.size, 8 * keep.size),
        name="add",
    )(keep, *came)


def halves_kernel(keep_ref, came_ref, *outs):
    rows = outs[0].shape[0]
    for half, out in enumerate(outs):
        part = pl.ds(half * rows, rows)
        out[...] = (keep_ref[part, :] + came_ref[part, :].astype(F32)).astype(out.dtype)


def add_halves(keep, came, dtypes):
    rows, block = keep.shape[0] // 2, keep.shape[1]
    return pl.pallas_call(
        halves_kernel,
        in_specs=[VECTORS] * 2,
        out_specs=[VECTORS] * 2,
        out_shape=[jax.ShapeDtypeStruct((rows, block), dtype) for dtype in dtypes],
        compiler_params=params(),
        cost_estimate=cost(keep.size, 9 * keep.size),
        name="halves",
    )(keep, came)


def total_kernel(both, downs, keep_ref, *refs):
    came, outs = refs[: len(refs) - 2], refs[len(refs) - 2 :]
    rows = outs[0].shape[0]
    for half, out in enumerate(outs):
        part = pl.ds(half * rows, rows)
        total = keep_ref[part, :]
        for ref in came[:both]:
            total = total + ref[part, :].astype(F32)
        for ref in came[both:][slice(downs) if half == 0 else slice(downs, None)]:
            total = total + ref[...].astype(F32)
        out[...] = total


def total(keep, both, downs, ups):
    rows, block = keep.shape[0] // 2, keep.shape[1]
    came = [*both, *downs, *ups]
    return pl.pallas_call(
        functools.partial(total_kernel, len(both), len(downs)),
        in_specs=[VECTORS] * (1 + len(came)),
        out_specs=[VECTORS] * 2,
        out_shape=[jax.ShapeDtypeStruct((rows, block), F32)] * 2,
        compiler_params=params(),
        cost_estimate=cost(keep.size * len(came), keep.size * (8 + 2 * len(came))),
        name="total",
    )(keep, *came)


def last_kernel(down_total, up_total, down_came, up_came, down_ref, up_ref):
    down_ref[...] = down_total[...] + down_came[...].astype(F32)
    up_ref[...] = up_total[...] + up_came[...].astype(F32)


def last(down, up, down_came, up_came):
    return pl.pallas_call(
        last_kernel,
        in_specs=[VECTORS] * 4,
        out_specs=[VECTORS] * 2,
        out_shape=[jax.ShapeDtypeStruct(down.shape, F32)] * 2,
        compiler_params=params(),
        cost_estimate=cost(2 * down.size, 20 * down.size),
        name="last",
    )(down, up, down_came, up_came)


def input_kernel(low_ref, own_ref, other_ref, out_ref):
    tile = out_ref.shape[1]
    rows = own_ref.shape[0]
    cols = pl.ds(pl.multiple_of(pl.program_id(0) * tile, 128), tile)
    dot = functools.partial(lax.dot_general, dimension_numbers=TN, preferred_element_type=F32)
    out_ref[...] = (
        dot(low_ref[:rows], other_ref[:, cols]) + dot(low_ref[rows:], own_ref[:, cols])
    ).astype(BF16)


def input_gradient(low, own, other):
    tokens = low.shape[1]
    rows, width = own.shape
    steps = steps_of(width)
    tile = width // steps
    return pl.pallas_call(
        input_kernel,
        grid=(steps,),
        in_specs=[VECTORS] * 3,
        out_specs=pl.BlockSpec((tokens, tile), lambda s: (0, s)),
        out_shape=jax.ShapeDtypeStruct((tokens, width), BF16),
        compiler_params=params(),
        cost_estimate=cost(4 * rows * tokens * width, 2 * (2 * rows + tokens) * width),
        name="input",
    )(low, own, other)


def shards(x, g, ids, gates, down_w, up_w):
    tokens, width = x.shape
    count, rank, _ = down_w.shape
    rows = count * rank
    replicas = lax.axis_size("dp")
    block = width // replicas
    core = lax.axis_index("adapter")
    a = down_w.reshape(rows, width)
    b = up_w.reshape(rows, width)
    ids, gates = ids.T, gates.T
    swap = lambda array: lax.ppermute(array, "adapter", SWAP)
    b_in = swap(b)
    flip = lambda array, by: lax.ppermute(array, "dp", [(i, i ^ by) for i in range(replicas)])
    steps = replicas // 2
    if steps < 2 or replicas & (replicas - 1) or block % 128:
        return plain(core, ids, gates, rank, x, g, a, b, swap(a), b_in, swap)

    a_in = swap(a)
    g_held, x_held = hold(g, x)
    order = list(reversed(range(steps)))
    places = Places(steps)
    lg, la, pair, keep = low_products(
        places, ids, gates, rank, b, b_in, a, a_in, g_held, x_held, 2 * block
    )
    rest = rest_products(places, lg, la, x_held, g_held, steps - 1, 2 * block)
    terms = [(keep, swap(pair))] + [(k, swap(p)) for p, k in zip(rest[::2], rest[1::2])]
    both, downs, ups = [], [], []
    for i, step in enumerate(order):
        send, own = fold(places, block, 0, *terms[i])
        got = flip(send, 1)
        if step == 0:
            both.append(got)
        elif step == 1:
            nearest = [flip(half, 2) for half in add_halves(own, got, (BF16, BF16))]
        elif steps != 4:
            both.append(flip(add(own, got), 2 * step))
        elif step == 3:
            passed = [flip(half, 2) for half in add_halves(own, got, (BF16, BF16))]
        else:
            mine = add_halves(own, got, (F32, F32))
            for half, came, into in zip(mine, passed, (downs, ups)):
                into.append(flip(add(half, came), 4))
    input_grad = input_gradient(lg, a, a_in)
    input_grad, both[-1] = lax.optimization_barrier((input_grad, both[-1]))
    down, up = last(*total(own, both, downs, ups), *nearest)
    return input_grad, down.reshape(count, rank, block), up.reshape(count, rank, block)


def plain(core, ids, gates, rank, x, g, a, b, a_in, b_in, swap):
    rows = a.shape[0]
    dot = functools.partial(lax.dot_general, preferred_element_type=F32)
    weight = gate_columns(core, ids, gates, 2 * rows, rank)
    both_a, both_b = jnp.concatenate([a, a_in]), jnp.concatenate([b, b_in])
    lg = (dot(both_b, g, NT) * weight).astype(BF16)
    la = (dot(both_a, x, NT) * weight).astype(BF16)
    input_grad = dot(lg, both_a, TN).astype(BF16)
    down = jnp.dot(lg, x, preferred_element_type=F32)
    up = jnp.dot(la, g, preferred_element_type=F32)
    own = jnp.concatenate([down[:rows], up[:rows]])
    other = jnp.concatenate([down[rows:], up[rows:]]).astype(BF16)
    total = lax.psum_scatter(
        own + swap(other).astype(F32), "dp", scatter_dimension=1, tiled=True
    ).reshape(2, rows // rank, rank, -1)
    return input_grad, total[0], total[1]


def solution(mesh):
    tok = P(("groups", "dp", "adapter"), None)
    return jax.shard_map(
        shards,
        mesh=mesh,
        in_specs=(tok, tok, tok, tok, P("adapter", None, None), P("adapter", None, None)),
        out_specs=(
            tok,
            P(("groups", "adapter"), None, "dp"),
            P(("groups", "adapter"), None, "dp"),
        ),
        check_vma=False,
    )
```
